256 devices in a mesh: row: 16 (over x, y_hi, core), col: 16 (over y_lo, z).
Axes of the slice: x: 4, y: 4 (y_hi: 2, y_lo: 2; y = y_hi * 2 + y_lo), z: 8, core: 2. Of those that a mesh axis runs over, the one named last changes fastest.
Arguments:
- pair_out: bfloat16 [512, 768, 128], P('row', 'col'), may hold values from -6 to 6
- pair_left: bfloat16 [512, 512, 128], P('col', 'row'), may hold values from -6 to 6
- pair_right: bfloat16 [512, 768, 128], P('row', 'col'), may hold values from -6 to 6
- ln_gain: float32 [128], replicated, may hold values from 0.1 to 1.9
- ln_bias: float32 [128], replicated, may hold values from -3 to 3
- w_left: bfloat16 [128, 256], replicated, may hold values from -0.5 to 0.5
- w_right: bfloat16 [128, 256], replicated, may hold values from -0.5 to 0.5
- w_gate: bfloat16 [128, 128], replicated, may hold values from -0.5 to 0.5
- w_out: bfloat16 [128, 128], replicated, may hold values from -0.5 to 0.5
- out_gain: float32 [128], replicated, may hold values from 0.1 to 1.9
- out_bias: float32 [128], replicated, may hold values from -3 to 3
- cotangent: bfloat16 [512, 768, 128], P('row', 'col'), may hold values from -6 to 6
Outputs:
- result: bfloat16 [512, 768, 128], P('row', 'col')
- grad_out: bfloat16 [512, 768, 128], P('row', 'col')
- grad_left: bfloat16 [512, 512, 128], P('col', 'row')
- grad_right: bfloat16 [512, 768, 128], P('row', 'col')
The draws below stay inside these ranges and needn't reach their ends.
All inputs are finite; a program needn't handle non-finite values.
Results may differ from the reference program's by a relative error of at most 0.025.
Values may be sent and summed in bfloat16 or wider, within the bound.
A program may use at most 128 MiB of HBM per device.

```python
import jax
import jax.numpy as jnp
from jax import lax

C = 128
H = 128
K = 512
I = 512
J = 768
N_ROW = 16
N_COL = 16


def shard_levels(own_key, dims, pieces, low, top_value):
    level, own = 1.0, jax.random.fold_in(own_key, 6)
    for dim, blocks in pieces:
        heights = jnp.exp(jax.random.uniform(jax.random.fold_in(own, dim), (blocks,), jnp.float32, low / len(pieces), top_value / len(pieces)))
        level = level * jnp.repeat(heights, dims[dim] // blocks).reshape([-1 if axis == dim else 1 for axis in range(len(dims))])
    return level


def gaussian(own_key, dims, scale, most, shards=(), held_as=jnp.bfloat16):
    array = jax.random.normal(own_key, dims, jnp.float32) * scale
    if len(shards) > 0:
        array = shard_levels(own_key, dims, shards, -0.22, 0.18) * array
    return jnp.clip(array, min=-most, max=most).astype(held_as)


def setup_inputs(seed: int = 0) -> dict:
    key_of = jax.random.split(jax.random.key(seed), 13)
    pair_out = gaussian(key_of[0], (I, J, C), 1.0, 6.0, ((0, 16), (1, 16)))
    pair_left = gaussian(key_of[1], (K, I, C), 1.0, 6.0, ((0, 16), (1, 16)))
    pair_right = gaussian(key_of[2], (K, J, C), 1.0, 6.0, ((0, 16), (1, 16)))
    ln_gain = jnp.clip(1.0 + 0.18 * jax.random.normal(key_of[3], (C,), jnp.float32), 0.1, 1.9)
    ln_bias = gaussian(key_of[4], (C,), 0.5, 3.0, (), jnp.float32)
    w_left = gaussian(key_of[5], (C, 2 * H), C ** -0.5, 0.5)
    w_right = gaussian(key_of[6], (C, 2 * H), C ** -0.5, 0.5)
    w_gate = gaussian(key_of[7], (C, C), C ** -0.5, 0.5)
    w_out = gaussian(key_of[8], (H, C), H ** -0.5, 0.5)
    out_gain = jnp.clip(1.0 + 0.18 * jax.random.normal(key_of[9], (H,), jnp.float32), 0.1, 1.9)
    out_bias = gaussian(key_of[10], (H,), 0.5, 3.0, (), jnp.float32)
    cotangent = gaussian(key_of[11], (I, J, C), 1.0, 6.0, ((0, 16), (1, 16)))
    return dict(pair_out=pair_out, pair_left=pair_left, pair_right=pair_right, ln_gain=ln_gain, ln_bias=ln_bias, w_left=w_left, w_right=w_right, w_gate=w_gate, w_out=w_out, out_gain=out_gain, out_bias=out_bias, cotangent=cotangent)


def normalize(values, gain, bias):
    center = values - lax.optimization_barrier(jnp.mean(values, axis=-1, keepdims=True))
    inverse = lax.rsqrt(lax.optimization_barrier(jnp.mean(center * center, axis=-1, keepdims=True)) + 1e-05)
    standard = center * inverse
    return (standard * gain + bias, standard, inverse)

def norm_back(upstream, standard, inverse, gain):
    scaled = upstream * gain
    return inverse * (scaled - lax.optimization_barrier(jnp.mean(scaled, axis=-1, keepdims=True)) - standard * lax.optimization_barrier(jnp.mean(scaled * standard, axis=-1, keepdims=True)))

def project(pair_tile, gain, bias, weight):
    normed, standard, inverse = normalize(pair_tile.astype(jnp.float32), gain, bias)
    normed = normed.astype(jnp.bfloat16)
    hidden_width = weight.shape[1] // 2
    pre_act = jnp.dot(normed.reshape(-1, normed.shape[-1]), weight, preferred_element_type=jnp.float32)
    pre_act = pre_act.reshape(pair_tile.shape[:-1] + (2 * hidden_width,))
    gated = (jax.nn.sigmoid(pre_act[..., hidden_width:]) * pre_act[..., :hidden_width]).astype(jnp.bfloat16)
    return (gated, pre_act, standard, inverse)

def project_back(d_gated, pre_act, standard, inverse, gain, weight):
    hidden_width = weight.shape[1] // 2
    squash = jax.nn.sigmoid(pre_act[..., hidden_width:])
    values_half = pre_act[..., :hidden_width]
    d_pre = jnp.concatenate([d_gated * squash, d_gated * values_half * squash * (1.0 - squash)], axis=-1)
    d_pre = d_pre.astype(jnp.bfloat16)
    d_normed = jnp.dot(d_pre.reshape(-1, 2 * hidden_width), weight.T, preferred_element_type=jnp.float32)
    return norm_back(d_normed.reshape(standard.shape), standard, inverse, gain).astype(jnp.bfloat16)

def reference(pair_out, pair_left, pair_right, ln_gain, ln_bias, w_left, w_right, w_gate, w_out, out_gain, out_bias, cotangent):
    left_gated, left_pre, left_std, left_inv = project(pair_left, ln_gain, ln_bias, w_left)
    right_gated, right_pre, right_std, right_inv = project(pair_right, ln_gain, ln_bias, w_right)
    triangle = jnp.einsum('kih,kjh->ijh', left_gated.astype(jnp.float32), right_gated.astype(jnp.float32), precision=lax.Precision.HIGHEST)
    tri_normed, tri_std, tri_inv = normalize(triangle, out_gain, out_bias)
    tri_normed = tri_normed.astype(jnp.bfloat16)
    out_normed, out_std, out_inv = normalize(pair_out.astype(jnp.float32), ln_gain, ln_bias)
    out_normed = out_normed.astype(jnp.bfloat16)
    out_gate = jax.nn.sigmoid(jnp.dot(out_normed.reshape(-1, C), w_gate, preferred_element_type=jnp.float32))
    out_proj = jnp.dot(tri_normed.reshape(-1, H), w_out, preferred_element_type=jnp.float32)
    result = (out_gate * out_proj).astype(jnp.bfloat16).reshape(I, J, C)
    upstream = cotangent.reshape(-1, C).astype(jnp.float32)
    d_proj = (upstream * out_gate).astype(jnp.bfloat16)
    d_gate = (upstream * out_proj * out_gate * (1.0 - out_gate)).astype(jnp.bfloat16)
    d_outn = jnp.dot(d_gate, w_gate.T, preferred_element_type=jnp.float32).reshape(I, J, C)
    grad_out = norm_back(d_outn, out_std, out_inv, ln_gain).astype(jnp.bfloat16)
    d_trin = jnp.dot(d_proj, w_out.T, preferred_element_type=jnp.float32).reshape(I, J, H)
    d_triangle = norm_back(d_trin, tri_std, tri_inv, out_gain).astype(jnp.bfloat16)
    col_width = J // N_COL
    grad_blocks = d_triangle.reshape(I, N_COL, col_width, H).transpose(1, 0, 2, 3)
    right_blocks = right_gated.reshape(K, N_COL, col_width, H).transpose(1, 0, 2, 3)

    def left_step(running, blocks):
        grad_block, right_block = blocks
        block_part = jnp.einsum('ijh,kjh->kih', grad_block.astype(jnp.float32), right_block.astype(jnp.float32), precision=lax.Precision.HIGHEST)
        block_part = lax.optimization_barrier(block_part.astype(jnp.bfloat16)).astype(jnp.float32)
        return (running + block_part, None)
    d_left, _ = lax.scan(left_step, jnp.zeros((K, I, H), jnp.float32), (grad_blocks, right_blocks))
    row_width = I // N_ROW
    grad_rowblocks = d_triangle.reshape(N_ROW, row_width, J, H)
    left_blocks = left_gated.reshape(K, N_ROW, row_width, H).transpose(1, 0, 2, 3)

    def right_step(running, blocks):
        grad_block, left_block = blocks
        block_part = jnp.einsum('ijh,kih->kjh', grad_block.astype(jnp.float32), left_block.astype(jnp.float32), precision=lax.Precision.HIGHEST)
        block_part = lax.optimization_barrier(block_part.astype(jnp.bfloat16)).astype(jnp.float32)
        return (running + block_part, None)
    d_right, _ = lax.scan(right_step, jnp.zeros((K, J, H), jnp.float32), (grad_rowblocks, left_blocks))
    grad_left = project_back(d_left, left_pre, left_std, left_inv, ln_gain, w_left)
    grad_right = project_back(d_right, right_pre, right_std, right_inv, ln_gain, w_right)
    return (result, grad_out, grad_left, grad_right)
```

```python
import jax
import jax.numpy as jnp
from jax import lax
from jax.experimental import pallas as pl
from jax.experimental.pallas import tpu as pltpu
from jax.sharding import PartitionSpec as P

MESH = pl.DeviceIdType.MESH
BF16 = jnp.bfloat16
F32 = jnp.float32
NZ = 8
PLANE = 32
HS = 4
EPS = 1e-05


def standardize(values):
    center = values - jnp.mean(values, axis=-1, keepdims=True)
    inverse = lax.rsqrt(jnp.mean(center * center, axis=-1, keepdims=True) + EPS)
    return center * inverse, inverse


def norm_back(upstream, standard, inverse, gain):
    scaled = upstream * gain
    return inverse * (
        scaled
        - jnp.mean(scaled, axis=-1, keepdims=True)
        - standard * jnp.mean(scaled * standard, axis=-1, keepdims=True)
    )


def dot_nn(a, b):
    return lax.dot_general(a, b, (((1,), (0,)), ((), ())), preferred_element_type=F32)


def dot_nt(a, b):
    return lax.dot_general(a, b, (((1,), (1,)), ((), ())), preferred_element_type=F32)


def swap64(x0, x1):
    low = lax.broadcasted_iota(jnp.int32, x0.shape, 1) < 64
    return (
        jnp.where(low, x0, pltpu.roll(x1, 64, 1)),
        jnp.where(low, pltpu.roll(x0, 64, 1), x1),
    )


def swap32(x0, x1):
    low = lax.broadcasted_iota(jnp.int32, x0.shape, 1) % 64 < 32
    return (
        jnp.where(low, x0, pltpu.roll(x1, 32, 1)),
        jnp.where(low, pltpu.roll(x0, 96, 1), x1),
    )


def exchange4(x):
    y0, y2 = swap64(x[0], x[2])
    y1, y3 = swap64(x[1], x[3])
    z0, z1 = swap32(y0, y1)
    z2, z3 = swap32(y2, y3)
    return z0, z1, z2, z3


def project_kernel(left, right, gain, bias, w_left, w_right, ls, rs, lpre, rpre, scr):
    g, bi = gain[...], bias[...]
    zeros = jnp.zeros((16, 128), F32)

    def rows_of(tile):
        standard, _ = standardize(tile.astype(F32))
        return standard * g + bi

    wl = w_left[...].T

    def left_step(a, _):
        normed = rows_of(jnp.concatenate([left[8 * b + a] for b in range(4)], axis=0))
        pre = dot_nt(wl, normed.astype(BF16))
        lpre[a] = pre
        scr[pl.ds(a, 128, stride=8), :] = jax.nn.sigmoid(pre[128:]) * pre[:128]
        return 0

    lax.fori_loop(0, 8, left_step, 0, unroll=2)
    ls[...] = scr[0:1024, :].astype(BF16).reshape(PLANE, 32, 128)

    wr = w_right[...].T

    def right_step(a, _):
        normed = rows_of(jnp.concatenate([right[a], right[16 + a]], axis=0))
        padded = jnp.concatenate([normed[:48], zeros, normed[48:], zeros], axis=0)
        pre = dot_nt(wr, padded.astype(BF16))
        rpre[a] = pre
        scr[pl.ds(a, 128, stride=16), :] = jax.nn.sigmoid(pre[128:]) * pre[:128]
        return 0

    lax.fori_loop(0, 16, right_step, 0, unroll=2)
    rs[...] = scr[...].astype(BF16).reshape(PLANE, 64, 128)


def project_back_kernel(dl, dr, left, right, lpre, rpre, gain, w_left, w_right, gl, gr, scr):
    g = gain[...]

    def back(d, pre, w, x):
        p, q = pre[:128], pre[128:]
        squash = jax.nn.sigmoid(q)
        d_pre = jnp.concatenate([d * squash, d * p * squash * (1.0 - squash)], axis=0)
        e = dot_nn(w, d_pre.astype(BF16)).T
        return e, x

    scr[0:1024, :] = dl[...].reshape(1024, 128).astype(F32)
    wl = w_left[...]

    def left_step(a, _):
        d = scr[pl.ds(a, 128, stride=8), :]
        x = jnp.concatenate([left[8 * b + a] for b in range(4)], axis=0).astype(F32)
        e, x = back(d, lpre[a], wl, x)
        standard, inverse = standardize(x)
        out = norm_back(e, standard, inverse, g).astype(BF16)
        for b in range(4):
            gl[8 * b + a] = out[32 * b : 32 * b + 32]
        return 0

    lax.fori_loop(0, 8, left_step, 0, unroll=2)

    scr[...] = dr[...].reshape(2048, 128).astype(F32)
    wr = w_right[...]

    def right_step(a, _):
        d = scr[pl.ds(a, 128, stride=16), :]
        x = jnp.concatenate([right[a], right[16 + a]], axis=0).astype(F32)
        e, x = back(d, rpre[a], wr, x)
        e = jnp.concatenate([e[0:48], e[64:112]], axis=0)
        standard, inverse = standardize(x)
        out = norm_back(e, standard, inverse, g).astype(BF16)
        gr[a] = out[:48]
        gr[16 + a] = out[48:]
        return 0

    lax.fori_loop(0, 16, right_step, 0, unroll=2)


FLOWS = ((1, 0, 4), (1, 1, 3), (-1, 0, 3), (-1, 1, 4))


def triangle_kernel(
    ls, rs, pair_out, cot, gain, bias, w_gate, w_out, o_gain, o_bias,
    result, grad_out, dl_out, dr_out,
    lbuf, rbuf, tsend, tbuf, dsend, dbuf, drsend, drbuf, dls, rsbuf, dlsend, dlbuf,
    lm, rm, dm, scr, big,
    a2a_send, a2a_recv, ag_send, ag_recv, rs_send, rs_recv,
):
    row = lax.axis_index("row")
    col = lax.axis_index("col")
    z = lax.rem(col, NZ)
    yl = col // NZ
    me = row * 2 + yl

    def plane_id(p):
        return {"row": p // 2, "col": lax.rem(p, 2) * NZ + z}

    def z_id(direction):
        return {"row": row, "col": yl * NZ + lax.rem(z + NZ + direction, NZ)}

    barrier = pltpu.get_barrier_semaphore()

    def greet(s, _):
        p = lax.rem(me + s, PLANE)
        pl.semaphore_signal(barrier, inc=1, device_id=plane_id(p), device_id_type=MESH)
        return 0

    lax.fori_loop(1, PLANE, greet, 0)
    for direction in (1, -1):
        pl.semaphore_signal(barrier, inc=1, device_id=z_id(direction), device_id_type=MESH)
    pl.semaphore_wait(barrier, PLANE - 1 + 2)

    def a2a_start(n, src, dst):
        pltpu.make_async_copy(src.at[me], dst.at[me], a2a_recv.at[n]).start()

        def send(s, _):
            p = lax.rem(me + s, PLANE)
            pltpu.make_async_remote_copy(
                src_ref=src.at[p], dst_ref=dst.at[me],
                send_sem=a2a_send.at[n], recv_sem=a2a_recv.at[n],
                device_id=plane_id(p), device_id_type=MESH,
            ).start()
            return 0

        lax.fori_loop(1, PLANE, send, 0)

    def a2a_wait(n, dst):
        pltpu.make_async_copy(dst, dst, a2a_recv.at[n]).wait()

    def a2a_drain(n, src):
        part = src.at[pl.ds(0, PLANE - 1)]
        pltpu.make_async_copy(part, part, a2a_send.at[n]).wait()

    def gather_copy(f, s):
        direction, half, _ = FLOWS[f]
        block = lbuf.at[lax.rem(z + NZ - direction * s, NZ), pl.ds(16 * half, 16)]
        return pltpu.make_async_remote_copy(
            src_ref=block, dst_ref=block,
            send_sem=ag_send.at[f, s], recv_sem=ag_recv.at[f, s],
            device_id=z_id(direction), device_id_type=MESH,
        )

    def unmix_left(zz):
        def step(n, _):
            ylk, q = n // 4, lax.rem(n, 4)
            x = [lbuf[zz, (4 * q + t) * 2 + ylk].astype(F32) for t in range(4)]
            y = exchange4(x)
            k0 = pl.multiple_of((ylk * NZ + zz) * 32, 32)
            lanes = pl.ds(pl.multiple_of(q * 128, 128), 128)
            for h in range(HS):
                block = jnp.concatenate([y[b][8 * h : 8 * h + 8] for b in range(4)], axis=0)
                lm[h, pl.ds(k0, 32), lanes] = block.astype(BF16)
            return 0

        lax.fori_loop(0, 8, step, 0)

    def unmix_pair(src, dst):
        def step(r, _):
            y = swap64(src[2 * r].astype(F32), src[2 * r + 1].astype(F32))
            r0 = pl.multiple_of(r * 32, 32)
            for h in range(HS):
                block = jnp.concatenate([y[g][16 * h : 16 * h + 16] for g in range(2)], axis=0)
                dst[h, pl.ds(r0, 32), :] = block.astype(BF16)
            return 0

        lax.fori_loop(0, 16, step, 0)

    def mix_pair(dst):
        def step(r, _):
            for h in range(HS):
                r0 = pl.multiple_of(h * 512 + r * 32, 32)
                y = swap64(scr[pl.ds(r0, 16), :], scr[pl.ds(r0 + 16, 16), :])
                for g in range(2):
                    dst[2 * r + g, 16 * h : 16 * h + 16, :] = y[g].astype(BF16)
            return 0

        lax.fori_loop(0, 16, step, 0)

    a2a_start(0, ls, lbuf.at[z])
    a2a_start(1, rs, rbuf)
    a2a_wait(0, lbuf.at[z])
    for f in range(4):
        gather_copy(f, 0).start()
    a2a_wait(1, rbuf)
    unmix_pair(rbuf, rm)
    unmix_left(z)
    for s in range(4):
        for f in range(4):
            if s < FLOWS[f][2]:
                gather_copy(f, s).wait_recv()
                if s + 1 < FLOWS[f][2]:
                    gather_copy(f, s + 1).start()
        if s < 3:
            unmix_left(lax.rem(z + NZ - s - 1, NZ))
            unmix_left(lax.rem(z + s + 1, NZ))
        else:
            unmix_left(lax.rem(z + 4, NZ))

    for h in range(HS):
        scr[512 * h : 512 * h + 512, :] = dot_nn(rm[h].T, lm[h]).T
    mix_pair(tsend)
    a2a_start(2, tsend, tbuf)
    a2a_wait(2, tbuf)

    scr[...] = tbuf[...].reshape(2048, 128).astype(F32)
    g_in, b_in, g_tri, b_tri = gain[...], bias[...], o_gain[...], o_bias[...]
    wg, wo = w_gate[...], w_out[...]
    zeros = jnp.zeros((16, 128), F32)

    def rows_step(a, _):
        tri = scr[pl.ds(a, 128, stride=16), :].T
        tri = jnp.concatenate([tri[0:48], tri[64:112]], axis=0)
        x = jnp.concatenate([pair_out[a], pair_out[16 + a]], axis=0).astype(F32)
        up = jnp.concatenate([cot[a], cot[16 + a]], axis=0).astype(F32)
        out_std, out_inv = standardize(x)
        gate = jax.nn.sigmoid(dot_nn((out_std * g_in + b_in).astype(BF16), wg))
        tri_std, tri_inv = standardize(tri)
        proj = dot_nn((tri_std * g_tri + b_tri).astype(BF16), wo)
        res = (gate * proj).astype(BF16)
        result[a] = res[:48]
        result[16 + a] = res[48:]
        d_proj = (up * gate).astype(BF16)
        d_gate = (up * proj * gate * (1.0 - gate)).astype(BF16)
        g_out = norm_back(dot_nt(d_gate, wg), out_std, out_inv, g_in).astype(BF16)
        grad_out[a] = g_out[:48]
        grad_out[16 + a] = g_out[48:]
        d_tri = norm_back(dot_nt(d_proj, wo), tri_std, tri_inv, g_tri)
        padded = jnp.concatenate([d_tri[:48], zeros, d_tri[48:], zeros], axis=0)
        scr[pl.ds(a, 128, stride=16), :] = padded.T
        return 0

    lax.fori_loop(0, 16, rows_step, 0)
    dsend[...] = scr[...].astype(BF16).reshape(PLANE, 64, 128)
    a2a_start(3, dsend, dbuf)
    a2a_wait(3, dbuf)
    unmix_pair(dbuf, dm)

    for h in range(HS):
        big[h] = dot_nt(rm[h], dm[h])

    def pack_left(c, _):
        k0 = pl.multiple_of(c * 32, 32)
        for q in range(4):
            x = [
                jnp.concatenate(
                    [big[h, pl.ds(k0 + 8 * b, 8), 128 * q : 128 * q + 128] for h in range(HS)],
                    axis=0,
                )
                for b in range(4)
            ]
            y = exchange4(x)
            for t in range(4):
                dls[lax.rem(c, NZ), (4 * q + t) * 2 + c // NZ] = y[t].astype(BF16)
        return 0

    lax.fori_loop(0, 16, pack_left, 0)

    def sum_copy(f, s):
        direction, half, steps = FLOWS[f]
        block = dls.at[lax.rem(z + NZ + direction * (steps - s), NZ), pl.ds(16 * half, 16)]
        return pltpu.make_async_remote_copy(
            src_ref=block, dst_ref=rsbuf.at[f, s],
            send_sem=rs_send.at[f, s], recv_sem=rs_recv.at[f, s],
            device_id=z_id(direction), device_id_type=MESH,
        )

    for f in range(4):
        sum_copy(f, 0).start()

    for h in range(HS):
        scr[512 * h : 512 * h + 512, :] = dot_nn(lm[h], dm[h])
    mix_pair(drsend)
    a2a_start(4, drsend, drbuf)

    for s in range(4):
        for f in range(4):
            direction, half, steps = FLOWS[f]
            if s < steps:
                sum_copy(f, s).wait_recv()
                if s + 1 < steps:
                    chunk = lax.rem(z + NZ + direction * (steps - s - 1), NZ)
                    here = (chunk, pl.ds(16 * half, 16))
                    dls[here] = (dls[here].astype(F32) + rsbuf[f, s].astype(F32)).astype(BF16)
                    sum_copy(f, s + 1).start()
    for half in range(2):
        here = pl.ds(16 * half, 16)
        total = dls[z, here].astype(F32)
        for f in range(4):
            if FLOWS[f][1] == half:
                total = total + rsbuf[f, FLOWS[f][2] - 1].astype(F32)
        dlsend[here] = total.astype(BF16)
    a2a_start(5, dlsend, dlbuf)
    a2a_wait(4, drbuf)
    dr_out[...] = drbuf[...]
    a2a_wait(5, dlbuf)
    dl_out[...] = dlbuf[...]

    for n, src in enumerate((ls, rs, tsend, dsend, drsend, dlsend)):
        a2a_drain(n, src)
    for f in range(4):
        for s in range(FLOWS[f][2]):
            gather_copy(f, s).wait_send()
            sum_copy(f, s).wait_send()


VMEM_LIMIT = 56 * 1024 * 1024


def per_device(
    pair_out, pair_left, pair_right, ln_gain, ln_bias, w_left, w_right, w_gate, w_out,
    out_gain, out_bias, cotangent,
):
    vm = pl.BlockSpec(memory_space=pltpu.VMEM)
    gain, bias = ln_gain.reshape(1, 128), ln_bias.reshape(1, 128)
    o_gain, o_bias = out_gain.reshape(1, 128), out_bias.reshape(1, 128)
    ls, rs, lpre, rpre = pl.pallas_call(
        project_kernel,
        out_shape=(
            jax.ShapeDtypeStruct((PLANE, 32, 128), BF16),
            jax.ShapeDtypeStruct((PLANE, 64, 128), BF16),
            jax.ShapeDtypeStruct((8, 256, 128), F32),
            jax.ShapeDtypeStruct((16, 256, 128), F32),
        ),
        in_specs=[vm] * 6,
        out_specs=(vm,) * 4,
        scratch_shapes=[pltpu.VMEM((2048, 128), F32)],
        compiler_params=pltpu.CompilerParams(vmem_limit_bytes=VMEM_LIMIT),
        name="project",
    )(pair_left, pair_right, gain, bias, w_left, w_right)

    half_slots = pltpu.VMEM((PLANE, 32, 128), BF16)
    slots = pltpu.VMEM((PLANE, 64, 128), BF16)
    dma = pltpu.SemaphoreType.DMA
    result, grad_out, dl, dr = pl.pallas_call(
        triangle_kernel,
        out_shape=(
            jax.ShapeDtypeStruct((32, 48, 128), BF16),
            jax.ShapeDtypeStruct((32, 48, 128), BF16),
            jax.ShapeDtypeStruct((PLANE, 32, 128), BF16),
            jax.ShapeDtypeStruct((PLANE, 64, 128), BF16),
        ),
        in_specs=[vm] * 10,
        out_specs=(vm,) * 4,
        scratch_shapes=[
            pltpu.VMEM((NZ, PLANE, 32, 128), BF16),
            slots,
            slots,
            slots,
            slots,
            slots,
            slots,
            slots,
            pltpu.VMEM((NZ, PLANE, 32, 128), BF16),
            pltpu.VMEM((4, 4, 16, 32, 128), BF16),
            half_slots,
            half_slots,
            pltpu.VMEM((HS, 512, 512), BF16),
            pltpu.VMEM((HS, 512, 128), BF16),
            pltpu.VMEM((HS, 512, 128), BF16),
            pltpu.VMEM((2048, 128), F32),
            pltpu.VMEM((HS, 512, 512), F32),
            dma((6,)), dma((6,)), dma((4, 4)), dma((4, 4)), dma((4, 4)), dma((4, 4)),
        ],
        compiler_params=pltpu.CompilerParams(
            vmem_limit_bytes=VMEM_LIMIT, collective_id=0, has_side_effects=True
        ),
        name="triangle",
    )(ls, rs, pair_out, cotangent, gain, bias, w_gate, w_out, o_gain, o_bias)

    grad_left, grad_right = pl.pallas_call(
        project_back_kernel,
        out_shape=(
            jax.ShapeDtypeStruct((32, 32, 128), BF16),
            jax.ShapeDtypeStruct((32, 48, 128), BF16),
        ),
        in_specs=[vm] * 9,
        out_specs=(vm,) * 2,
        scratch_shapes=[pltpu.VMEM((2048, 128), F32)],
        compiler_params=pltpu.CompilerParams(vmem_limit_bytes=VMEM_LIMIT),
        name="project_back",
    )(dl, dr, pair_left, pair_right, lpre, rpre, gain, w_left, w_right)
    return result, grad_out, grad_left, grad_right


def solution(mesh):
    pairs, lefts = P("row", "col", None), P("col", "row", None)
    return jax.shard_map(
        per_device,
        mesh=mesh,
        in_specs=(pairs, lefts, pairs, P(), P(), P(), P(), P(), P(), P(), P(), pairs),
        out_specs=(pairs, pairs, lefts, pairs),
        check_vma=False,
    )
```

```python
import jax
import jax.numpy as jnp
from jax import lax
from jax.experimental import pallas as pl
from jax.experimental.pallas import tpu as pltpu
from jax.sharding import PartitionSpec as P

MESH = pl.DeviceIdType.MESH
BF16 = jnp.bfloat16
F32 = jnp.float32
NZ = 8
PLANE = 32
HALF = PLANE // 2
HS = 4
EPS = 1e-05


def cat(parts, axis=0):
    return jnp.concatenate(parts, axis=axis)


def standardize(values):
    center = values - jnp.mean(values, axis=-1, keepdims=True)
    inverse = lax.rsqrt(jnp.mean(center * center, axis=-1, keepdims=True) + EPS)
    return center * inverse, inverse


def norm_back(upstream, standard, inverse, gain):
    scaled = upstream * gain
    return inverse * (
        scaled
        - jnp.mean(scaled, axis=-1, keepdims=True)
        - standard * jnp.mean(scaled * standard, axis=-1, keepdims=True)
    )


def dot_nn(a, b):
    return lax.dot_general(a, b, (((1,), (0,)), ((), ())), preferred_element_type=F32)


def dot_nt(a, b):
    return lax.dot_general(a, b, (((1,), (1,)), ((), ())), preferred_element_type=F32)


def swap64(x0, x1):
    low = lax.broadcasted_iota(jnp.int32, x0.shape, 1) < 64
    return (
        jnp.where(low, x0, pltpu.roll(x1, 64, 1)),
        jnp.where(low, pltpu.roll(x0, 64, 1), x1),
    )


def swap32(x0, x1):
    low = lax.broadcasted_iota(jnp.int32, x0.shape, 1) % 64 < 32
    return (
        jnp.where(low, x0, pltpu.roll(x1, 32, 1)),
        jnp.where(low, pltpu.roll(x0, 96, 1), x1),
    )


def exchange4(x):
    y0, y2 = swap64(x[0], x[2])
    y1, y3 = swap64(x[1], x[3])
    z0, z1 = swap32(y0, y1)
    z2, z3 = swap32(y2, y3)
    return z0, z1, z2, z3


def project_left(left, g, bi, w, ls, lpre, scr):
    x = cat([left[8 * b + a] for a in range(8) for b in range(4)]).astype(F32)
    standard, _ = standardize(x)
    pre = dot_nt(w.T, (standard * g + bi).astype(BF16))
    gated = jax.nn.sigmoid(pre[128:]) * pre[:128]
    for a in range(8):
        lpre[a] = pre[:, 128 * a : 128 * a + 128]
        scr[pl.ds(a, 128, stride=8), :] = gated[:, 128 * a : 128 * a + 128]
    ls[...] = scr[0:1024, :].astype(BF16).reshape(PLANE, 32, 128)


def project_right(right, g, bi, w, rs, rpre, scr):
    zeros = jnp.zeros((16, 128), F32)
    wr = w.T

    def step(n, _):
        x = cat([right[16 * b + n * 8 + t] for t in range(8) for b in range(2)]).astype(F32)
        standard, _ = standardize(x)
        normed = standard * g + bi
        normed = cat([y for t in range(16) for y in (normed[48 * t : 48 * t + 48], zeros)])
        pre = dot_nt(wr, normed.astype(BF16))
        gated = jax.nn.sigmoid(pre[128:]) * pre[:128]
        for t in range(8):
            rpre[n * 8 + t] = pre[:, 128 * t : 128 * t + 128]
            scr[pl.ds(n * 8 + t, 128, stride=16), :] = gated[:, 128 * t : 128 * t + 128]
        return 0

    lax.fori_loop(0, 2, step, 0)
    rs[...] = scr[...].astype(BF16).reshape(PLANE, 64, 128)


def gate_rows(pair_out, g, bi, wg, gate_s, std_s, inv_s):
    def step(n, _):
        x = cat([pair_out[16 * b + n * 8 + t] for t in range(8) for b in range(2)]).astype(F32)
        standard, inverse = standardize(x)
        rows = pl.ds(pl.multiple_of(n * 768, 768), 768)
        gate_s[rows, :] = jax.nn.sigmoid(dot_nn((standard * g + bi).astype(BF16), wg))
        std_s[rows, :] = standard
        inv_s[rows, :] = jnp.broadcast_to(inverse, standard.shape)
        return 0

    lax.fori_loop(0, 2, step, 0)


def slab_rows(n, scr, scr2, cot, g_in, g_tri, b_tri, wg, wo, gate_s, std_s, inv_s, result, grad_out):
    zeros = jnp.zeros((16, 128), F32)
    parts = []
    for t in range(8):
        tri = scr[pl.ds(n * 8 + t, 128, stride=16), :].T
        parts += [tri[0:48], tri[64:112]]
    tri = cat(parts)
    up = cat([cot[16 * b + n * 8 + t] for t in range(8) for b in range(2)]).astype(F32)
    rows = pl.ds(n * 768, 768)
    gate, out_std, out_inv = gate_s[rows, :], std_s[rows, :], inv_s[rows, :]
    tri_std, tri_inv = standardize(tri)
    proj = dot_nn((tri_std * g_tri + b_tri).astype(BF16), wo)
    gated_up = up * gate
    d_tri = norm_back(dot_nt(gated_up.astype(BF16), wo), tri_std, tri_inv, g_tri)
    res = (gate * proj).astype(BF16)
    d_gate = (gated_up * proj * (1.0 - gate)).astype(BF16)
    g_out = norm_back(dot_nt(d_gate, wg), out_std, out_inv, g_in).astype(BF16)
    for t in range(8):
        for b in range(2):
            o = (2 * t + b) * 48
            result[16 * b + n * 8 + t] = res[o : o + 48]
            grad_out[16 * b + n * 8 + t] = g_out[o : o + 48]
        o = 96 * t
        padded = cat([d_tri[o : o + 48], zeros, d_tri[o + 48 : o + 96], zeros])
        scr2[pl.ds(n * 8 + t, 128, stride=16), :] = padded.T


def d_pre_of(d, pre):
    p, q = pre[:128], pre[128:]
    squash = jax.nn.sigmoid(q)
    d_p = d * squash
    return cat([d_p, d_p * p * (1.0 - squash)]).astype(BF16)


def back_left(left, lpre, g, w, gl, scr):
    d = cat([scr[pl.ds(a, 128, stride=8), :] for a in range(8)], axis=1)
    pre = cat([lpre[a] for a in range(8)], axis=1)
    e = dot_nn(w, d_pre_of(d, pre)).T
    x = cat([left[8 * b + a] for a in range(8) for b in range(4)]).astype(F32)
    standard, inverse = standardize(x)
    out = norm_back(e, standard, inverse, g).astype(BF16)
    for a in range(8):
        for b in range(4):
            o = 128 * a + 32 * b
            gl[8 * b + a] = out[o : o + 32]


def back_right(n, right, rpre, g, w, gr, scr):
    d = cat([scr[pl.ds(n * 8 + t, 128, stride=16), :] for t in range(8)], axis=1)
    pre = cat([rpre[n * 8 + t] for t in range(8)], axis=1)
    e = dot_nn(w, d_pre_of(d, pre)).T
    e = cat([y for t in range(8) for y in (e[128 * t : 128 * t + 48], e[128 * t + 64 : 128 * t + 112])])
    x = cat([right[16 * b + n * 8 + t] for t in range(8) for b in range(2)]).astype(F32)
    standard, inverse = standardize(x)
    out = norm_back(e, standard, inverse, g).astype(BF16)
    for t in range(8):
        for b in range(2):
            o = (2 * t + b) * 48
            gr[16 * b + n * 8 + t] = out[o : o + 48]


FLOWS = ((1, 0, 4), (1, 1, 3), (-1, 0, 3), (-1, 1, 4))
QUART = HALF // 2


def triangle_kernel(
    left_hbm, right_hbm, out_hbm, cot_hbm, gain, bias, w_left, w_right, w_gate, w_out, o_gain, o_bias,
    result_hbm, grad_out_hbm, grad_left_hbm, grad_right_hbm,
    left, right, pair_out, cot, result, grad_out, grad_left, grad_right,
    ls, rs, lpre, rpre, gate_s, std_s, inv_s,
    lbuf, rbuf, tsend, tbuf, dsend, dbuf, drsend, drbuf, dls, rsbuf, dlsend, dlbuf,
    lm, rm, rmt, dm, scr, scr2, big,
    in_sem, out_sem, a2a_send, a2a_recv, ag_send, ag_recv, rs_send, rs_recv,
):
    row = lax.axis_index("row")
    col = lax.axis_index("col")
    z = lax.rem(col, NZ)
    yl = col // NZ
    core = lax.rem(row, 2)
    me16 = (row // 2) * 2 + yl
    me = core * HALF + me16

    def plane_id(p):
        q = lax.rem(p, HALF)
        return {"row": (q // 2) * 2 + p // HALF, "col": lax.rem(q, 2) * NZ + z}

    def z_id(direction):
        return {"row": row, "col": yl * NZ + lax.rem(z + NZ + direction, NZ)}

    barrier = pltpu.get_barrier_semaphore()

    def greet(s, _):
        p = lax.rem(me + s, PLANE)
        pl.semaphore_signal(barrier, inc=1, device_id=plane_id(p), device_id_type=MESH)
        return 0

    lax.fori_loop(1, PLANE, greet, 0)
    for direction in (1, -1):
        pl.semaphore_signal(barrier, inc=1, device_id=z_id(direction), device_id_type=MESH)

    loads = [
        pltpu.make_async_copy(src, dst, in_sem.at[n])
        for n, (src, dst) in enumerate(
            ((left_hbm, left), (right_hbm, right), (out_hbm, pair_out), (cot_hbm, cot))
        )
    ]
    stores = [
        pltpu.make_async_copy(src, dst, out_sem.at[n])
        for n, (src, dst) in enumerate(
            (
                (result, result_hbm),
                (grad_out, grad_out_hbm),
                (grad_left, grad_left_hbm),
                (grad_right, grad_right_hbm),
            )
        )
    ]
    for load in loads:
        load.start()

    def remote(n, src, dst, p):
        return pltpu.make_async_remote_copy(
            src_ref=src, dst_ref=dst.at[me],
            send_sem=a2a_send.at[n], recv_sem=a2a_recv.at[n],
            device_id=plane_id(p), device_id_type=MESH,
        )

    def all_start(n, src, dst, slot):
        pltpu.make_async_copy(src.at[me], dst.at[slot], a2a_recv.at[n]).start()

        def send(s, _):
            p = lax.rem(me + s, PLANE)
            pltpu.make_async_remote_copy(
                src_ref=src.at[p], dst_ref=dst.at[slot],
                send_sem=a2a_send.at[n], recv_sem=a2a_recv.at[n],
                device_id=plane_id(p), device_id_type=MESH,
            ).start()
            return 0

        lax.fori_loop(1, PLANE, send, 0)

    def all_drain(n, src):
        part = src.at[pl.ds(0, PLANE - 1)]
        pltpu.make_async_copy(part, part, a2a_send.at[n]).wait()

    def part_start(n, kappa, src, dst):
        @pl.when(core == kappa)
        def _():
            pltpu.make_async_copy(src.at[me16], dst.at[me], a2a_recv.at[n]).start()

        @pl.when(core != kappa)
        def _():
            remote(n, src.at[me16], dst, kappa * HALF + me16).start()

        def send(s, _):
            d = lax.rem(me16 + s, HALF)
            remote(n, src.at[d], dst, kappa * HALF + d).start()
            return 0

        lax.fori_loop(1, HALF, send, 0)

    def part_drain(n, kappa, src):
        @pl.when(core == kappa)
        def _():
            part = src.at[pl.ds(0, HALF - 1)]
            pltpu.make_async_copy(part, part, a2a_send.at[n]).wait()

        @pl.when(core != kappa)
        def _():
            pltpu.make_async_copy(src, src, a2a_send.at[n]).wait()

    def arrived(n, dst):
        pltpu.make_async_copy(dst, dst, a2a_recv.at[n]).wait()

    def z_slots(kappa, half):
        return pl.ds(HALF * kappa + QUART * half, QUART)

    def gather_copy(kappa, f, s):
        direction, half, _ = FLOWS[f]
        block = lbuf.at[lax.rem(z + NZ - direction * s, NZ), z_slots(kappa, half)]
        return pltpu.make_async_remote_copy(
            src_ref=block, dst_ref=block,
            send_sem=ag_send.at[kappa, f, s], recv_sem=ag_recv.at[kappa, f, s],
            device_id=z_id(direction), device_id_type=MESH,
        )

    def gather_start(kappa):
        for f in range(4):
            gather_copy(kappa, f, 0).start()

    def gather_pump(kappa, s):
        for f in range(4):
            if s < FLOWS[f][2]:
                gather_copy(kappa, f, s).wait_recv()
                if s + 1 < FLOWS[f][2]:
                    gather_copy(kappa, f, s + 1).start()

    def unmix_left(kappa, zz):
        def step(n, _):
            ylk, q = n // 2, lax.rem(n, 2)
            x = [lbuf[zz, HALF * kappa + (4 * q + t) * 2 + ylk].astype(F32) for t in range(4)]
            y = exchange4(x)
            k0 = pl.multiple_of((ylk * NZ + zz) * 32, 32)
            lanes = pl.ds(pl.multiple_of(256 * kappa + q * 128, 128), 128)
            for h in range(HS):
                block = cat([y[b][8 * h : 8 * h + 8] for b in range(4)])
                lm[h, pl.ds(k0, 32), lanes] = block.astype(BF16)
            return 0

        lax.fori_loop(0, 4, step, 0, unroll=2)

    def unmix_gathered(kappa, s):
        if s < 3:
            unmix_left(kappa, lax.rem(z + NZ - s - 1, NZ))
            unmix_left(kappa, lax.rem(z + s + 1, NZ))
        else:
            unmix_left(kappa, lax.rem(z + 4, NZ))

    def unmix_pair(src, first, count, put):
        def step(m, _):
            y = swap64(src[first + 2 * m].astype(F32), src[first + 2 * m + 1].astype(F32))
            for h in range(HS):
                put(h, m, cat([y[g][16 * h : 16 * h + 16] for g in range(2)]).astype(BF16))
            return 0

        lax.fori_loop(0, count, step, 0, unroll=2)

    def unmix_right():
        for kappa in range(2):

            def put(h, m, block):
                rm[h, pl.ds(pl.multiple_of((2 * m + kappa) * 32, 32), 32), :] = block

            unmix_pair(rbuf, HALF * kappa, 8, put)

    def unmix_d(kappa):
        def put(h, m, block):
            dm[h, pl.ds(pl.multiple_of(256 * kappa + m * 32, 32), 32), :] = block

        unmix_pair(dbuf, HALF * kappa, 8, put)

    def mix_pair(per_channel, blocks, put):
        def step(m, _):
            for h in range(HS):
                r0 = pl.multiple_of(h * per_channel + m * 32, 32)
                y = swap64(scr[pl.ds(r0, 16), :], scr[pl.ds(r0 + 16, 16), :])
                for v in range(2):
                    put(m, v, h, y[v].astype(BF16))
            return 0

        lax.fori_loop(0, blocks, step, 0, unroll=2)

    def triangle(kappa):
        for h in range(HS):
            scr[256 * h : 256 * h + 256, :] = dot_nn(rmt[h], lm[h, :, 256 * kappa : 256 * kappa + 256]).T

        def put(m, v, h, block):
            tsend[kappa, 2 * m + v, 16 * h : 16 * h + 16, :] = block

        mix_pair(256, 8, put)
        part_start(2 + kappa, kappa, tsend.at[kappa], tbuf)

    g_in, b_in, g_tri, b_tri = gain[...], bias[...], o_gain[...], o_bias[...]
    wg, wo = w_gate[...], w_out[...]

    def slab(kappa, n):
        @pl.when(core == kappa)
        def _():
            if n == 0:
                arrived(2 + kappa, tbuf)
                scr[...] = tbuf[...].reshape(2048, 128).astype(F32)
            slab_rows(
                n, scr, scr2, cot, g_in, g_tri, b_tri, wg, wo, gate_s, std_s, inv_s, result, grad_out
            )
            if n == 1:
                dsend[...] = scr2[...].astype(BF16).reshape(PLANE, 64, 128)
                all_start(4 + kappa, dsend, dbuf, me)
                stores[0].start()
                stores[1].start()

    def sum_copy(kappa, f, s):
        direction, half, steps = FLOWS[f]
        block = dls.at[lax.rem(z + NZ + direction * (steps - s), NZ), z_slots(kappa, half)]
        return pltpu.make_async_remote_copy(
            src_ref=block, dst_ref=rsbuf.at[kappa, f, s],
            send_sem=rs_send.at[kappa, f, s], recv_sem=rs_recv.at[kappa, f, s],
            device_id=z_id(direction), device_id_type=MESH,
        )

    def left_sums(kappa):
        arrived(4 + kappa, dbuf.at[pl.ds(HALF * kappa, HALF)])
        unmix_d(kappa)
        for h in range(HS):
            big[h] = dot_nt(rm[h], dm[h, 256 * kappa : 256 * kappa + 256, :])

        def pack(c, _):
            k0 = pl.multiple_of(c * 32, 32)
            for q in range(2):
                x = [
                    cat([big[h, pl.ds(k0 + 8 * b, 8), 128 * q : 128 * q + 128] for h in range(HS)])
                    for b in range(4)
                ]
                y = exchange4(x)
                for t in range(4):
                    slot = HALF * kappa + (4 * q + t) * 2 + c // NZ
                    dls[lax.rem(c, NZ), slot] = y[t].astype(BF16)
            return 0

        lax.fori_loop(0, 16, pack, 0, unroll=2)
        for f in range(4):
            sum_copy(kappa, f, 0).start()

    def sum_pump(kappa, s):
        for f in range(4):
            direction, half, steps = FLOWS[f]
            if s < steps:
                sum_copy(kappa, f, s).wait_recv()
                if s + 1 < steps:
                    here = (lax.rem(z + NZ + direction * (steps - s - 1), NZ), z_slots(kappa, half))
                    dls[here] = (dls[here].astype(F32) + rsbuf[kappa, f, s].astype(F32)).astype(BF16)
                    sum_copy(kappa, f, s + 1).start()

    def left_out(kappa):
        for half in range(2):
            total = dls[z, z_slots(kappa, half)].astype(F32)
            for f in range(4):
                if FLOWS[f][1] == half:
                    total = total + rsbuf[kappa, f, FLOWS[f][2] - 1].astype(F32)
            dlsend[kappa, QUART * half : QUART * half + QUART] = total.astype(BF16)
        part_start(7 + kappa, kappa, dlsend.at[kappa], dlbuf)

    loads[0].wait()
    project_left(left, g_in, b_in, w_left[...], ls, lpre, scr)
    pl.semaphore_wait(barrier, PLANE - 1 + 2)
    all_start(0, ls, lbuf.at[z], me)
    loads[1].wait()
    project_right(right, g_in, b_in, w_right[...], rs, rpre, scr2)
    all_start(1, rs, rbuf, me)
    arrived(0, lbuf.at[z])
    gather_start(0)
    loads[2].wait()
    gate_rows(pair_out, g_in, b_in, wg, gate_s, std_s, inv_s)
    unmix_left(0, z)
    unmix_left(1, z)
    gather_pump(0, 0)
    unmix_gathered(0, 0)
    arrived(1, rbuf)
    gather_pump(0, 1)
    unmix_right()
    for h in range(HS):
        rmt[h] = rm[h].T
    unmix_gathered(0, 1)
    gather_pump(0, 2)
    gather_start(1)
    unmix_gathered(0, 2)
    gather_pump(0, 3)
    unmix_gathered(0, 3)
    loads[3].wait()

    triangle(0)
    gather_pump(1, 0)
    unmix_gathered(1, 0)
    gather_pump(1, 1)
    unmix_gathered(1, 1)
    slab(0, 0)
    gather_pump(1, 2)
    unmix_gathered(1, 2)
    slab(0, 1)
    gather_pump(1, 3)
    unmix_gathered(1, 3)
    triangle(1)

    left_sums(0)
    slab(1, 0)
    sum_pump(0, 0)
    slab(1, 1)
    sum_pump(0, 1)
    sum_pump(0, 2)
    left_sums(1)
    sum_pump(0, 3)
    left_out(0)

    for h in range(HS):
        scr[512 * h : 512 * h + 512, :] = dot_nn(lm[h], dm[h])

    def put_right(m, v, h, block):
        drsend[lax.rem(m, 2) * HALF + (m // 2) * 2 + v, 16 * h : 16 * h + 16, :] = block

    mix_pair(512, 16, put_right)
    all_start(6, drsend, drbuf, me)
    sum_pump(1, 0)
    sum_pump(1, 1)
    arrived(6, drbuf)
    scr[...] = drbuf[...].reshape(2048, 128).astype(F32)
    wr = w_right[...]
    back_right(0, right, rpre, g_in, wr, grad_right, scr)
    sum_pump(1, 2)
    back_right(1, right, rpre, g_in, wr, grad_right, scr)
    stores[3].start()
    sum_pump(1, 3)
    left_out(1)
    for kappa in range(2):

        @pl.when(core == kappa)
        def _():
            arrived(7 + kappa, dlbuf)

    scr[0:1024, :] = dlbuf[...].reshape(1024, 128).astype(F32)
    back_left(left, lpre, g_in, w_left[...], grad_left, scr)
    stores[2].start()

    all_drain(0, ls)
    all_drain(1, rs)
    all_drain(6, drsend)
    for kappa in range(2):
        part_drain(2 + kappa, kappa, tsend.at[kappa])
        part_drain(7 + kappa, kappa, dlsend.at[kappa])

        @pl.when(core == kappa)
        def _():
            all_drain(4 + kappa, dsend)

        for f in range(4):
            for s in range(FLOWS[f][2]):
                gather_copy(kappa, f, s).wait_send()
                sum_copy(kappa, f, s).wait_send()
    for store in stores:
        store.wait()


def hand_over_kernel(*refs):
    count = len(refs) // 2
    sems = refs[-1]
    copies = [pltpu.make_async_copy(refs[n], refs[count + n], sems.at[n]) for n in range(count)]
    for copy in copies:
        copy.start()
    for copy in copies:
        copy.wait()


VMEM_LIMIT = 56 * 1024 * 1024


def per_device(
    pair_out, pair_left, pair_right, ln_gain, ln_bias, w_left, w_right, w_gate, w_out,
    out_gain, out_bias, cotangent,
):
    vm = pl.BlockSpec(memory_space=pltpu.VMEM)
    hbm = pl.BlockSpec(memory_space=pl.ANY)
    gain, bias = ln_gain.reshape(1, 128), ln_bias.reshape(1, 128)
    o_gain, o_bias = out_gain.reshape(1, 128), out_bias.reshape(1, 128)

    def vmem(*shape, dtype=BF16):
        return pltpu.VMEM(shape, dtype)

    def wide(*shape):
        return pltpu.VMEM(shape, F32)

    pair, lefts = (32, 48, 128), (32, 32, 128)
    slots, half_slots = vmem(PLANE, 64, 128), vmem(PLANE, 32, 128)
    dma = pltpu.SemaphoreType.DMA
    outs = tuple(jax.ShapeDtypeStruct(shape, BF16) for shape in (pair, pair, lefts, pair))
    made = pl.pallas_call(
        triangle_kernel,
        out_shape=outs,
        in_specs=[hbm] * 4 + [vm] * 8,
        out_specs=(hbm,) * 4,
        scratch_shapes=[
            vmem(*lefts), vmem(*pair), vmem(*pair), vmem(*pair),
            vmem(*pair), vmem(*pair), vmem(*lefts), vmem(*pair),
            half_slots, slots,
            wide(8, 256, 128), wide(16, 256, 128),
            wide(1536, 128), wide(1536, 128), wide(1536, 128),
            vmem(NZ, PLANE, 32, 128), slots,
            vmem(2, HALF, 64, 128), slots,
            slots, slots,
            slots, slots,
            vmem(NZ, PLANE, 32, 128), vmem(2, 4, 4, QUART, 32, 128),
            vmem(2, HALF, 32, 128), half_slots,
            vmem(HS, 512, 512), vmem(HS, 512, 128),
            vmem(HS, 128, 512), vmem(HS, 512, 128),
            wide(2048, 128), wide(2048, 128), wide(HS, 512, 256),
            dma((4,)), dma((4,)), dma((9,)), dma((9,)),
            dma((2, 4, 4)), dma((2, 4, 4)), dma((2, 4, 4)), dma((2, 4, 4)),
        ],
        compiler_params=pltpu.CompilerParams(
            vmem_limit_bytes=VMEM_LIMIT, collective_id=0, has_side_effects=True
        ),
        name="triangle",
    )(
        pair_left, pair_right, pair_out, cotangent, gain, bias, w_left, w_right, w_gate, w_out,
        o_gain, o_bias,
    )
    return pl.pallas_call(
        hand_over_kernel,
        out_shape=outs,
        in_specs=[hbm] * 4,
        out_specs=(hbm,) * 4,
        scratch_shapes=[dma((4,))],
        compiler_params=pltpu.CompilerParams(vmem_limit_bytes=VMEM_LIMIT),
        name="hand_over",
    )(*made)


def solution(mesh):
    pairs, lefts = P("row", "col", None), P("col", "row", None)
    return jax.shard_map(
        per_device,
        mesh=mesh,
        in_specs=(pairs, lefts, pairs, P(), P(), P(), P(), P(), P(), P(), P(), pairs),
        out_specs=(pairs, pairs, lefts, pairs),
        check_vma=False,
    )
```

```python
import jax
import jax.numpy as jnp
from jax import lax
from jax.experimental import pallas as pl
from jax.experimental.pallas import tpu as pltpu
from jax.sharding import PartitionSpec as P

MESH = pl.DeviceIdType.MESH
BF16 = jnp.bfloat16
F32 = jnp.float32
NZ = 8
PLANE = 32
HALF = PLANE // 2
HS = 4
EPS = 1e-05


def cat(parts, axis=0):
    return jnp.concatenate(parts, axis=axis)


def standardize(values):
    center = values - jnp.mean(values, axis=-1, keepdims=True)
    inverse = lax.rsqrt(jnp.mean(center * center, axis=-1, keepdims=True) + EPS)
    return center * inverse, inverse


def norm_back(upstream, standard, inverse, gain):
    scaled = upstream * gain
    return inverse * (
        scaled
        - jnp.mean(scaled, axis=-1, keepdims=True)
        - standard * jnp.mean(scaled * standard, axis=-1, keepdims=True)
    )


def dot_nn(a, b):
    return lax.dot_general(a, b, (((1,), (0,)), ((), ())), preferred_element_type=F32)


def dot_nt(a, b):
    return lax.dot_general(a, b, (((1,), (1,)), ((), ())), preferred_element_type=F32)


def swap64(x0, x1):
    low = lax.broadcasted_iota(jnp.int32, x0.shape, 1) < 64
    return (
        jnp.where(low, x0, pltpu.roll(x1, 64, 1)),
        jnp.where(low, pltpu.roll(x0, 64, 1), x1),
    )


def swap32(x0, x1):
    low = lax.broadcasted_iota(jnp.int32, x0.shape, 1) % 64 < 32
    return (
        jnp.where(low, x0, pltpu.roll(x1, 32, 1)),
        jnp.where(low, pltpu.roll(x0, 96, 1), x1),
    )


def exchange4(x):
    y0, y2 = swap64(x[0], x[2])
    y1, y3 = swap64(x[1], x[3])
    z0, z1 = swap32(y0, y1)
    z2, z3 = swap32(y2, y3)
    return z0, z1, z2, z3


def project_left(left, g, bi, w, ls, lpre, scr):
    x = cat([left[8 * b + a] for a in range(8) for b in range(4)]).astype(F32)
    standard, _ = standardize(x)
    pre = dot_nt(w.T, (standard * g + bi).astype(BF16))
    gated = jax.nn.sigmoid(pre[128:]) * pre[:128]
    for a in range(8):
        lpre[a] = pre[:, 128 * a : 128 * a + 128]
        scr[pl.ds(a, 128, stride=8), :] = gated[:, 128 * a : 128 * a + 128]
    ls[...] = scr[0:1024, :].astype(BF16).reshape(PLANE, 32, 128)


def project_right(right, g, bi, w, rs, rpre, scr):
    zeros = jnp.zeros((16, 128), F32)
    wr = w.T

    def step(n, _):
        x = cat([right[16 * b + n * 8 + t] for t in range(8) for b in range(2)]).astype(F32)
        standard, _ = standardize(x)
        normed = standard * g + bi
        normed = cat([y for t in range(16) for y in (normed[48 * t : 48 * t + 48], zeros)])
        pre = dot_nt(wr, normed.astype(BF16))
        gated = jax.nn.sigmoid(pre[128:]) * pre[:128]
        for t in range(8):
            rpre[n * 8 + t] = pre[:, 128 * t : 128 * t + 128]
            scr[pl.ds(n * 8 + t, 128, stride=16), :] = gated[:, 128 * t : 128 * t + 128]
        return 0

    lax.fori_loop(0, 2, step, 0)
    rs[...] = scr[...].astype(BF16).reshape(PLANE, 64, 128)


def gate_rows(pair_out, g, bi, wg, gate_s, std_s, inv_s):
    def step(n, _):
        x = cat([pair_out[16 * b + n * 8 + t] for t in range(8) for b in range(2)]).astype(F32)
        standard, inverse = standardize(x)
        rows = pl.ds(pl.multiple_of(n * 768, 768), 768)
        gate_s[rows, :] = jax.nn.sigmoid(dot_nn((standard * g + bi).astype(BF16), wg))
        std_s[rows, :] = standard
        inv_s[rows, :] = jnp.broadcast_to(inverse, standard.shape)
        return 0

    lax.fori_loop(0, 2, step, 0)


def slab_rows(n, scr, scr2, cot, g_in, g_tri, b_tri, wg, wo, gate_s, std_s, inv_s, result, grad_out):
    zeros = jnp.zeros((16, 128), F32)
    parts = []
    for t in range(8):
        tri = scr[pl.ds(n * 8 + t, 128, stride=16), :].T
        parts += [tri[0:48], tri[64:112]]
    tri = cat(parts)
    up = cat([cot[16 * b + n * 8 + t] for t in range(8) for b in range(2)]).astype(F32)
    rows = pl.ds(n * 768, 768)
    gate, out_std, out_inv = gate_s[rows, :], std_s[rows, :], inv_s[rows, :]
    tri_std, tri_inv = standardize(tri)
    proj = dot_nn((tri_std * g_tri + b_tri).astype(BF16), wo)
    gated_up = up * gate
    d_tri = norm_back(dot_nt(gated_up.astype(BF16), wo), tri_std, tri_inv, g_tri)
    res = (gate * proj).astype(BF16)
    d_gate = (gated_up * proj * (1.0 - gate)).astype(BF16)
    g_out = norm_back(dot_nt(d_gate, wg), out_std, out_inv, g_in).astype(BF16)
    for t in range(8):
        for b in range(2):
            o = (2 * t + b) * 48
            result[16 * b + n * 8 + t] = res[o : o + 48]
            grad_out[16 * b + n * 8 + t] = g_out[o : o + 48]
        o = 96 * t
        padded = cat([d_tri[o : o + 48], zeros, d_tri[o + 48 : o + 96], zeros])
        scr2[pl.ds(n * 8 + t, 128, stride=16), :] = padded.T


def d_pre_of(d, pre):
    p, q = pre[:128], pre[128:]
    squash = jax.nn.sigmoid(q)
    d_p = d * squash
    return cat([d_p, d_p * p * (1.0 - squash)]).astype(BF16)


def back_left(left, lpre, g, w, gl, scr):
    d = cat([scr[pl.ds(a, 128, stride=8), :] for a in range(8)], axis=1)
    pre = cat([lpre[a] for a in range(8)], axis=1)
    e = dot_nn(w, d_pre_of(d, pre)).T
    x = cat([left[8 * b + a] for a in range(8) for b in range(4)]).astype(F32)
    standard, inverse = standardize(x)
    out = norm_back(e, standard, inverse, g).astype(BF16)
    for a in range(8):
        for b in range(4):
            o = 128 * a + 32 * b
            gl[8 * b + a] = out[o : o + 32]


def back_right(n, right, rpre, g, w, gr, scr):
    d = cat([scr[pl.ds(n * 8 + t, 128, stride=16), :] for t in range(8)], axis=1)
    pre = cat([rpre[n * 8 + t] for t in range(8)], axis=1)
    e = dot_nn(w, d_pre_of(d, pre)).T
    e = cat([y for t in range(8) for y in (e[128 * t : 128 * t + 48], e[128 * t + 64 : 128 * t + 112])])
    x = cat([right[16 * b + n * 8 + t] for t in range(8) for b in range(2)]).astype(F32)
    standard, inverse = standardize(x)
    out = norm_back(e, standard, inverse, g).astype(BF16)
    for t in range(8):
        for b in range(2):
            o = (2 * t + b) * 48
            gr[16 * b + n * 8 + t] = out[o : o + 48]


FLOWS = tuple(
    (direction, part, 4 if (part < 2) == (direction > 0) else 3)
    for part in range(4)
    for direction in (1, -1)
)
NF = len(FLOWS)
CHIPS = tuple((dx, dy, dl) for dx in (2, 1, 3, 0) for dy in (1, 0) for dl in (1, 0))
QUART = HALF // 4


def triangle_kernel(
    left_hbm, right_hbm, out_hbm, cot_hbm, gain, bias, w_left, w_right, w_gate, w_out, o_gain, o_bias,
    result_hbm, grad_out_hbm, grad_left_hbm, grad_right_hbm,
    left, right, pair_out, cot, result, grad_out, grad_left, grad_right,
    ls, rs, lpre, rpre, gate_s, std_s, inv_s,
    lbuf, rbuf, tsend, tbuf, dsend, dbuf, drsend, drbuf, dls, rsbuf, dlsend, dlbuf,
    lm, rm, rmt, dm, scr, scr2, big,
    in_sem, out_sem, a2a_send, a2a_recv, ag_send, ag_recv, rs_send, rs_recv,
):
    row = lax.axis_index("row")
    col = lax.axis_index("col")
    z = lax.rem(col, NZ)
    yl = col // NZ
    core = lax.rem(row, 2)
    me16 = (row // 2) * 2 + yl
    me = core * HALF + me16

    zs = [z] + [lax.rem(z + k, NZ) for k in range(1, NZ)]
    x0, yh0 = row // 4, lax.rem(row // 2, 2)
    xs = [x0] + [lax.rem(x0 + k, 4) for k in range(1, 4)]
    yhs, yls, cores = (yh0, 1 - yh0), (yl, 1 - yl), (core, 1 - core)

    def slot_of(dx, dy, dl):
        return xs[dx] * 4 + yhs[dy] * 2 + yls[dl]

    def plane_id(dx, dy, dl, core_there):
        return {"row": xs[dx] * 4 + yhs[dy] * 2 + core_there, "col": yls[dl] * NZ + z}

    def z_id(direction):
        return {"row": row, "col": yl * NZ + zs[direction % NZ]}

    barrier = pltpu.get_barrier_semaphore()

    for dx, dy, dl in CHIPS:
        for dc in range(2):
            if (dx, dy, dl, dc) != (0, 0, 0, 0):
                there = plane_id(dx, dy, dl, cores[dc])
                pl.semaphore_signal(barrier, inc=1, device_id=there, device_id_type=MESH)
    for direction in (1, -1):
        pl.semaphore_signal(barrier, inc=1, device_id=z_id(direction), device_id_type=MESH)

    loads = [
        pltpu.make_async_copy(src, dst, in_sem.at[n])
        for n, (src, dst) in enumerate(
            ((left_hbm, left), (right_hbm, right), (out_hbm, pair_out), (cot_hbm, cot))
        )
    ]
    stores = [
        pltpu.make_async_copy(src, dst, out_sem.at[n])
        for n, (src, dst) in enumerate(
            (
                (result, result_hbm),
                (grad_out, grad_out_hbm),
                (grad_left, grad_left_hbm),
                (grad_right, grad_right_hbm),
            )
        )
    ]
    for load in loads:
        load.start()

    def remote(n, src, dst, there):
        return pltpu.make_async_remote_copy(
            src_ref=src, dst_ref=dst,
            send_sem=a2a_send.at[n], recv_sem=a2a_recv.at[n],
            device_id=there, device_id_type=MESH,
        )

    def all_start(n, src, dst, slot):
        pltpu.make_async_copy(src.at[me], dst.at[slot], a2a_recv.at[n]).start()

        for dx, dy, dl in CHIPS:
            for dc in range(2):
                if (dx, dy, dl, dc) != (0, 0, 0, 0):
                    p = cores[dc] * HALF + slot_of(dx, dy, dl)
                    remote(n, src.at[p], dst.at[slot], plane_id(dx, dy, dl, cores[dc])).start()

    def all_drain(n, src):
        part = src.at[pl.ds(0, PLANE - 1)]
        pltpu.make_async_copy(part, part, a2a_send.at[n]).wait()

    def part_start(n, kappa, src, dst):
        @pl.when(core == kappa)
        def _():
            pltpu.make_async_copy(src.at[me16], dst.at[me], a2a_recv.at[n]).start()

        @pl.when(core != kappa)
        def _():
            remote(n, src.at[me16], dst.at[me], plane_id(0, 0, 0, kappa)).start()

        for dx, dy, dl in CHIPS:
            if (dx, dy, dl) != (0, 0, 0):
                there = plane_id(dx, dy, dl, kappa)
                remote(n, src.at[slot_of(dx, dy, dl)], dst.at[me], there).start()

    def part_drain(n, kappa, src):
        @pl.when(core == kappa)
        def _():
            part = src.at[pl.ds(0, HALF - 1)]
            pltpu.make_async_copy(part, part, a2a_send.at[n]).wait()

        @pl.when(core != kappa)
        def _():
            pltpu.make_async_copy(src, src, a2a_send.at[n]).wait()

    def arrived(n, dst):
        pltpu.make_async_copy(dst, dst, a2a_recv.at[n]).wait()

    def z_slots(kappa, part):
        return pl.ds(HALF * kappa + QUART * part, QUART)

    def gather_copy(kappa, f, s):
        direction, part, _ = FLOWS[f]
        block = lbuf.at[zs[-direction * s % NZ], z_slots(kappa, part)]
        return pltpu.make_async_remote_copy(
            src_ref=block, dst_ref=block,
            send_sem=ag_send.at[kappa, f, s], recv_sem=ag_recv.at[kappa, f, s],
            device_id=z_id(direction), device_id_type=MESH,
        )

    def gather_start(kappa):
        for f in range(NF):
            gather_copy(kappa, f, 0).start()

    def gather_pump(kappa, s):
        for f in range(NF):
            if s < FLOWS[f][2]:
                gather_copy(kappa, f, s).wait_recv()
                if s + 1 < FLOWS[f][2]:
                    gather_copy(kappa, f, s + 1).start()

    def unmix_left(kappa, zz):
        for n in range(4):
            ylk, q = n // 2, n % 2
            x = [lbuf[zz, HALF * kappa + (4 * q + t) * 2 + ylk].astype(F32) for t in range(4)]
            y = exchange4(x)
            k0 = pl.multiple_of((ylk * NZ + zz) * 32, 32)
            lanes = pl.ds(256 * kappa + q * 128, 128)
            for h in range(HS):
                block = cat([y[b][8 * h : 8 * h + 8] for b in range(4)])
                lm[h, pl.ds(k0, 32), lanes] = block.astype(BF16)

    def unmix_gathered(kappa, s):
        if s < 3:
            unmix_left(kappa, zs[NZ - s - 1])
            unmix_left(kappa, zs[s + 1])
        else:
            unmix_left(kappa, zs[4])

    def unmix_pair(src, first, count, put):
        for m in range(count):
            y = swap64(src[first + 2 * m].astype(F32), src[first + 2 * m + 1].astype(F32))
            for h in range(HS):
                put(h, m, cat([y[g][16 * h : 16 * h + 16] for g in range(2)]).astype(BF16))

    def unmix_right():
        for kappa in range(2):

            def put(h, m, block):
                rm[h, pl.ds((2 * m + kappa) * 32, 32), :] = block

            unmix_pair(rbuf, HALF * kappa, 8, put)

    def unmix_d(kappa):
        def put(h, m, block):
            dm[h, pl.ds(256 * kappa + m * 32, 32), :] = block

        unmix_pair(dbuf, HALF * kappa, 8, put)

    def mix_pair(per_channel, blocks, put):
        for m in range(blocks):
            for h in range(HS):
                r0 = h * per_channel + m * 32
                y = swap64(scr[pl.ds(r0, 16), :], scr[pl.ds(r0 + 16, 16), :])
                for v in range(2):
                    put(m, v, h, y[v].astype(BF16))

    def triangle(kappa):
        for h in range(HS):
            scr[256 * h : 256 * h + 256, :] = dot_nn(rmt[h], lm[h, :, 256 * kappa : 256 * kappa + 256]).T

        def put(m, v, h, block):
            tsend[kappa, 2 * m + v, 16 * h : 16 * h + 16, :] = block

        mix_pair(256, 8, put)
        part_start(2 + kappa, kappa, tsend.at[kappa], tbuf)

    g_in, b_in, g_tri, b_tri = gain[...], bias[...], o_gain[...], o_bias[...]
    wg, wo = w_gate[...], w_out[...]

    def slab(kappa, n):
        @pl.when(core == kappa)
        def _():
            if n == 0:
                arrived(2 + kappa, tbuf)
                scr[...] = tbuf[...].reshape(2048, 128).astype(F32)
            slab_rows(
                n, scr, scr2, cot, g_in, g_tri, b_tri, wg, wo, gate_s, std_s, inv_s, result, grad_out
            )
            if n == 1:
                dsend[...] = scr2[...].astype(BF16).reshape(PLANE, 64, 128)
                all_start(4 + kappa, dsend, dbuf, me)
                stores[0].start()
                stores[1].start()

    def sum_copy(kappa, f, s):
        direction, part, steps = FLOWS[f]
        block = dls.at[zs[direction * (steps - s) % NZ], z_slots(kappa, part)]
        return pltpu.make_async_remote_copy(
            src_ref=block, dst_ref=rsbuf.at[kappa, f, s],
            send_sem=rs_send.at[kappa, f, s], recv_sem=rs_recv.at[kappa, f, s],
            device_id=z_id(direction), device_id_type=MESH,
        )

    def left_sums(kappa):
        arrived(4 + kappa, dbuf.at[pl.ds(HALF * kappa, HALF)])
        unmix_d(kappa)
        for h in range(HS):
            big[h] = dot_nt(rm[h], dm[h, 256 * kappa : 256 * kappa + 256, :])

        def pack(c, _):
            k0 = pl.multiple_of(c * 32, 32)
            for q in range(2):
                x = [
                    cat([big[h, pl.ds(k0 + 8 * b, 8), 128 * q : 128 * q + 128] for h in range(HS)])
                    for b in range(4)
                ]
                y = exchange4(x)
                for t in range(4):
                    slot = HALF * kappa + (4 * q + t) * 2 + c // NZ
                    dls[lax.rem(c, NZ), slot] = y[t].astype(BF16)
            return 0

        lax.fori_loop(0, 16, pack, 0, unroll=2)
        for f in range(NF):
            sum_copy(kappa, f, 0).start()

    def sum_pump(kappa, s):
        for f in range(NF):
            direction, part, steps = FLOWS[f]
            if s < steps:
                sum_copy(kappa, f, s).wait_recv()
                if s + 1 < steps:
                    here = (zs[direction * (steps - s - 1) % NZ], z_slots(kappa, part))
                    dls[here] = (dls[here].astype(F32) + rsbuf[kappa, f, s].astype(F32)).astype(BF16)
                    sum_copy(kappa, f, s + 1).start()

    def left_out(kappa):
        for part in range(4):
            total = dls[z, z_slots(kappa, part)].astype(F32)
            for f in range(NF):
                if FLOWS[f][1] == part:
                    total = total + rsbuf[kappa, f, FLOWS[f][2] - 1].astype(F32)
            dlsend[kappa, QUART * part : QUART * part + QUART] = total.astype(BF16)
        part_start(7 + kappa, kappa, dlsend.at[kappa], dlbuf)

    loads[0].wait()
    project_left(left, g_in, b_in, w_left[...], ls, lpre, scr)
    pl.semaphore_wait(barrier, PLANE - 1 + 2)
    all_start(0, ls, lbuf.at[z], me)
    loads[1].wait()
    project_right(right, g_in, b_in, w_right[...], rs, rpre, scr2)
    arrived(0, lbuf.at[z])
    gather_start(0)
    all_start(1, rs, rbuf, me)
    loads[2].wait()
    unmix_left(0, z)
    unmix_left(1, z)
    gather_pump(0, 0)
    gather_start(1)
    gate_rows(pair_out, g_in, b_in, wg, gate_s, std_s, inv_s)
    unmix_gathered(0, 0)
    gather_pump(0, 1)
    gather_pump(1, 0)
    unmix_gathered(0, 1)
    unmix_gathered(1, 0)
    gather_pump(0, 2)
    gather_pump(1, 1)
    arrived(1, rbuf)
    unmix_right()
    for h in range(HS):
        rmt[h] = rm[h].T
    unmix_gathered(0, 2)
    gather_pump(0, 3)
    unmix_gathered(0, 3)
    loads[3].wait()

    triangle(0)
    gather_pump(1, 2)
    unmix_gathered(1, 1)
    unmix_gathered(1, 2)
    gather_pump(1, 3)
    unmix_gathered(1, 3)
    triangle(1)

    slab(0, 0)
    slab(0, 1)
    slab(1, 0)
    slab(1, 1)
    left_sums(0)
    sum_pump(0, 0)
    sum_pump(0, 1)
    left_sums(1)
    sum_pump(0, 2)
    sum_pump(1, 0)
    sum_pump(0, 3)
    left_out(0)

    for h in range(HS):
        scr[512 * h : 512 * h + 512, :] = dot_nn(lm[h], dm[h])

    def put_right(m, v, h, block):
        drsend[(m % 2) * HALF + (m // 2) * 2 + v, 16 * h : 16 * h + 16, :] = block

    mix_pair(512, 16, put_right)
    sum_pump(1, 1)
    all_start(6, drsend, drbuf, me)
    sum_pump(1, 2)
    sum_pump(1, 3)
    left_out(1)
    arrived(6, drbuf)
    scr[...] = drbuf[...].reshape(2048, 128).astype(F32)
    wr = w_right[...]
    back_right(0, right, rpre, g_in, wr, grad_right, scr)
    back_right(1, right, rpre, g_in, wr, grad_right, scr)
    stores[3].start()
    for kappa in range(2):

        @pl.when(core == kappa)
        def _():
            arrived(7 + kappa, dlbuf)

    scr[0:1024, :] = dlbuf[...].reshape(1024, 128).astype(F32)
    back_left(left, lpre, g_in, w_left[...], grad_left, scr)
    stores[2].start()

    all_drain(0, ls)
    all_drain(1, rs)
    all_drain(6, drsend)
    for kappa in range(2):
        part_drain(2 + kappa, kappa, tsend.at[kappa])
        part_drain(7 + kappa, kappa, dlsend.at[kappa])

        @pl.when(core == kappa)
        def _():
            all_drain(4 + kappa, dsend)

        for f in range(NF):
            for s in range(FLOWS[f][2]):
                gather_copy(kappa, f, s).wait_send()
                sum_copy(kappa, f, s).wait_send()
    for store in stores:
        store.wait()


def hand_over_kernel(*refs):
    srcs, dsts, held = refs[:4], refs[4:8], refs[8:12]
    in_sem, out_sem = refs[12:]
    ins = [pltpu.make_async_copy(srcs[n], held[n], in_sem.at[n]) for n in range(4)]
    outs = [pltpu.make_async_copy(held[n], dsts[n], out_sem.at[n]) for n in range(4)]
    for copy in ins:
        copy.start()
    for n in range(4):
        ins[n].wait()
        outs[n].start()
    for copy in outs:
        copy.wait()


VMEM_LIMIT = 56 * 1024 * 1024


def per_device(
    pair_out, pair_left, pair_right, ln_gain, ln_bias, w_left, w_right, w_gate, w_out,
    out_gain, out_bias, cotangent,
):
    vm = pl.BlockSpec(memory_space=pltpu.VMEM)
    hbm = pl.BlockSpec(memory_space=pl.ANY)
    gain, bias = ln_gain.reshape(1, 128), ln_bias.reshape(1, 128)
    o_gain, o_bias = out_gain.reshape(1, 128), out_bias.reshape(1, 128)

    def vmem(*shape, dtype=BF16):
        return pltpu.VMEM(shape, dtype)

    def wide(*shape):
        return pltpu.VMEM(shape, F32)

    pair, lefts = (32, 48, 128), (32, 32, 128)
    slots, half_slots = vmem(PLANE, 64, 128), vmem(PLANE, 32, 128)
    dma = pltpu.SemaphoreType.DMA
    outs = tuple(jax.ShapeDtypeStruct(shape, BF16) for shape in (pair, pair, lefts, pair))
    made = pl.pallas_call(
        triangle_kernel,
        out_shape=outs,
        in_specs=[hbm] * 4 + [vm] * 8,
        out_specs=(hbm,) * 4,
        scratch_shapes=[
            vmem(*lefts), vmem(*pair), vmem(*pair), vmem(*pair),
            vmem(*pair), vmem(*pair), vmem(*lefts), vmem(*pair),
            half_slots, slots,
            wide(8, 256, 128), wide(16, 256, 128),
            wide(1536, 128), wide(1536, 128), wide(1536, 128),
            vmem(NZ, PLANE, 32, 128), slots,
            vmem(2, HALF, 64, 128), slots,
            slots, slots,
            slots, slots,
            vmem(NZ, PLANE, 32, 128), vmem(2, NF, 4, QUART, 32, 128),
            vmem(2, HALF, 32, 128), half_slots,
            vmem(HS, 512, 512), vmem(HS, 512, 128),
            vmem(HS, 128, 512), vmem(HS, 512, 128),
            wide(2048, 128), wide(2048, 128), wide(HS, 512, 256),
            dma((4,)), dma((4,)), dma((9,)), dma((9,)),
            dma((2, NF, 4)), dma((2, NF, 4)), dma((2, NF, 4)), dma((2, NF, 4)),
        ],
        compiler_params=pltpu.CompilerParams(
            vmem_limit_bytes=VMEM_LIMIT, collective_id=0, has_side_effects=True
        ),
        name="triangle",
    )(
        pair_left, pair_right, pair_out, cotangent, gain, bias, w_left, w_right, w_gate, w_out,
        o_gain, o_bias,
    )
    return pl.pallas_call(
        hand_over_kernel,
        out_shape=outs,
        in_specs=[hbm] * 4,
        out_specs=(hbm,) * 4,
        scratch_shapes=[vmem(*pair), vmem(*pair), vmem(*lefts), vmem(*pair), dma((4,)), dma((4,))],
        compiler_params=pltpu.CompilerParams(vmem_limit_bytes=VMEM_LIMIT),
        name="hand_over",
    )(*made)


def solution(mesh):
    pairs, lefts = P("row", "col", None), P("col", "row", None)
    return jax.shard_map(
        per_device,
        mesh=mesh,
        in_specs=(pairs, lefts, pairs, P(), P(), P(), P(), P(), P(), P(), P(), pairs),
        out_specs=(pairs, pairs, lefts, pairs),
        check_vma=False,
    )
```

```python
import jax
import jax.numpy as jnp
from jax import lax
from jax.experimental import pallas as pl
from jax.experimental.pallas import tpu as pltpu
from jax.sharding import PartitionSpec as P

MESH = pl.DeviceIdType.MESH
BF16 = jnp.bfloat16
F32 = jnp.float32
NZ = 8
PLANE = 32
HALF = PLANE // 2
HS = 4
EPS = 1e-05


def cat(parts, axis=0):
    return jnp.concatenate(parts, axis=axis)


def standardize(values):
    center = values - jnp.mean(values, axis=-1, keepdims=True)
    inverse = lax.rsqrt(jnp.mean(center * center, axis=-1, keepdims=True) + EPS)
    return center * inverse, inverse


def norm_back(upstream, standard, inverse, gain):
    scaled = upstream * gain
    return inverse * (
        scaled
        - jnp.mean(scaled, axis=-1, keepdims=True)
        - standard * jnp.mean(scaled * standard, axis=-1, keepdims=True)
    )


def dot_nn(a, b):
    return lax.dot_general(a, b, (((1,), (0,)), ((), ())), preferred_element_type=F32)


def dot_nt(a, b):
    return lax.dot_general(a, b, (((1,), (1,)), ((), ())), preferred_element_type=F32)


def swap64(x0, x1):
    low = lax.broadcasted_iota(jnp.int32, x0.shape, 1) < 64
    return (
        jnp.where(low, x0, pltpu.roll(x1, 64, 1)),
        jnp.where(low, pltpu.roll(x0, 64, 1), x1),
    )


def swap32(x0, x1):
    low = lax.broadcasted_iota(jnp.int32, x0.shape, 1) % 64 < 32
    return (
        jnp.where(low, x0, pltpu.roll(x1, 32, 1)),
        jnp.where(low, pltpu.roll(x0, 96, 1), x1),
    )


def exchange4(x):
    y0, y2 = swap64(x[0], x[2])
    y1, y3 = swap64(x[1], x[3])
    z0, z1 = swap32(y0, y1)
    z2, z3 = swap32(y2, y3)
    return z0, z1, z2, z3


def gate_of(pre):
    squash = jax.nn.sigmoid(pre[128:])
    gated = squash * pre[:128]
    return gated, cat([squash, gated * (1.0 - squash)])


def project_left(left, g, bi, w, ls, lfac, scr):
    x = cat([left[8 * b + a] for a in range(8) for b in range(4)]).astype(F32)
    standard, _ = standardize(x)
    pre = dot_nt(w.T, (standard * g + bi).astype(BF16))
    gated, factors = gate_of(pre)
    for a in range(8):
        lfac[a] = factors[:, 128 * a : 128 * a + 128]
        scr[pl.ds(a, 128, stride=8), :] = gated[:, 128 * a : 128 * a + 128]
    ls[...] = scr[0:1024, :].astype(BF16).reshape(PLANE, 32, 128)


def project_right(right, g, bi, w, rs, rfac, scr):
    zeros = jnp.zeros((16, 128), F32)
    wr = w.T

    def step(n, _):
        x = cat([right[16 * b + n * 8 + t] for t in range(8) for b in range(2)]).astype(F32)
        standard, _ = standardize(x)
        normed = standard * g + bi
        normed = cat([y for t in range(16) for y in (normed[48 * t : 48 * t + 48], zeros)])
        pre = dot_nt(wr, normed.astype(BF16))
        gated, factors = gate_of(pre)
        for t in range(8):
            rfac[n * 8 + t] = factors[:, 128 * t : 128 * t + 128]
            scr[pl.ds(n * 8 + t, 128, stride=16), :] = gated[:, 128 * t : 128 * t + 128]
        return 0

    lax.fori_loop(0, 2, step, 0)
    rs[...] = scr[...].astype(BF16).reshape(PLANE, 64, 128)


def gate_rows(pair_out, cot, g, bi, wg, wo, g_tri, gate_s, std_s, inv_s, up_s):
    def step(n, _):
        x = cat([pair_out[16 * b + n * 8 + t] for t in range(8) for b in range(2)]).astype(F32)
        standard, inverse = standardize(x)
        rows = pl.ds(pl.multiple_of(n * 768, 768), 768)
        gate = jax.nn.sigmoid(dot_nn((standard * g + bi).astype(BF16), wg))
        up = cat([cot[16 * b + n * 8 + t] for t in range(8) for b in range(2)]).astype(F32)
        scaled = dot_nt((up * gate).astype(BF16), wo) * g_tri
        up_s[rows, :] = scaled - jnp.mean(scaled, axis=-1, keepdims=True)
        gate_s[rows, :] = gate
        std_s[rows, :] = standard
        inv_s[rows, :] = jnp.broadcast_to(inverse, standard.shape)
        return 0

    lax.fori_loop(0, 2, step, 0)


def slab_back(n, scr, scr2, up_s, tri_s):
    zeros = jnp.zeros((16, 128), F32)
    parts = []
    for t in range(8):
        tri = scr[pl.ds(n * 8 + t, 128, stride=16), :].T
        parts += [tri[0:48], tri[64:112]]
    tri_std, tri_inv = standardize(cat(parts))
    rows = pl.ds(n * 768, 768)
    tri_s[rows, :] = tri_std
    up = up_s[rows, :]
    d_tri = tri_inv * (up - tri_std * jnp.mean(up * tri_std, axis=-1, keepdims=True))
    for t in range(8):
        o = 96 * t
        padded = cat([d_tri[o : o + 48], zeros, d_tri[o + 48 : o + 96], zeros])
        scr2[pl.ds(n * 8 + t, 128, stride=16), :] = padded.T


def slab_rows(cot, g_in, g_tri, b_tri, wg, wo, gate_s, std_s, inv_s, tri_s, result, grad_out):
    def step(n, _):
        rows = pl.ds(pl.multiple_of(n * 768, 768), 768)
        up = cat([cot[16 * b + n * 8 + t] for t in range(8) for b in range(2)]).astype(F32)
        gate = gate_s[rows, :]
        proj = dot_nn((tri_s[rows, :] * g_tri + b_tri).astype(BF16), wo)
        res = (gate * proj).astype(BF16)
        d_gate = (up * gate * proj * (1.0 - gate)).astype(BF16)
        g_out = norm_back(dot_nt(d_gate, wg), std_s[rows, :], inv_s[rows, :], g_in).astype(BF16)
        for t in range(8):
            for b in range(2):
                o = (2 * t + b) * 48
                result[16 * b + n * 8 + t] = res[o : o + 48]
                grad_out[16 * b + n * 8 + t] = g_out[o : o + 48]
        return 0

    lax.fori_loop(0, 2, step, 0)


def d_pre_of(d, factors):
    return cat([d * factors[:128], d * factors[128:]]).astype(BF16)


def prepare_left(left, lstd, linv):
    x = cat([left[8 * b + a] for a in range(8) for b in range(4)]).astype(F32)
    standard, inverse = standardize(x)
    lstd[...] = standard
    linv[...] = jnp.broadcast_to(inverse, standard.shape)


def back_left(lstd, linv, lfac, g, w, gl, scr):
    d = cat([scr[pl.ds(a, 128, stride=8), :] for a in range(8)], axis=1)
    factors = cat([lfac[a] for a in range(8)], axis=1)
    e = dot_nn(w, d_pre_of(d, factors)).T
    out = norm_back(e, lstd[...], linv[...], g).astype(BF16)
    for a in range(8):
        for b in range(4):
            o = 128 * a + 32 * b
            gl[8 * b + a] = out[o : o + 32]


def back_right(n, right, rfac, g, w, gr, scr):
    d = cat([scr[pl.ds(n * 8 + t, 128, stride=16), :] for t in range(8)], axis=1)
    factors = cat([rfac[n * 8 + t] for t in range(8)], axis=1)
    e = dot_nn(w, d_pre_of(d, factors)).T
    e = cat([y for t in range(8) for y in (e[128 * t : 128 * t + 48], e[128 * t + 64 : 128 * t + 112])])
    x = cat([right[16 * b + n * 8 + t] for t in range(8) for b in range(2)]).astype(F32)
    standard, inverse = standardize(x)
    out = norm_back(e, standard, inverse, g).astype(BF16)
    for t in range(8):
        for b in range(2):
            o = (2 * t + b) * 48
            gr[16 * b + n * 8 + t] = out[o : o + 48]


FLOWS = tuple(
    (direction, part, 4 if (part < 2) == (direction > 0) else 3)
    for part in range(4)
    for direction in (1, -1)
)
NF = len(FLOWS)
CHIPS = tuple((dx, dy, dl) for dx in (2, 1, 3, 0) for dy in (1, 0) for dl in (1, 0))
QUART = HALF // 4


def triangle_kernel(
    left_hbm, right_hbm, out_hbm, cot_hbm, gain, bias, w_left, w_right, w_gate, w_out, o_gain, o_bias,
    result_hbm, grad_out_hbm, grad_left_hbm, grad_right_hbm,
    left, right, pair_out, cot, result, grad_out, grad_left, grad_right,
    ls, rs, lfac, rfac, gate_s, std_s, inv_s, up_s, tri_s, lstd, linv,
    lbuf, rbuf, tsend, tbuf, dsend, dbuf, drsend, drbuf, dls, rsbuf, dlsend, dlbuf,
    lm, rm, rmt, dm, scr, scr2, big,
    in_sem, out_sem, a2a_send, a2a_recv, ag_send, ag_recv, rs_send, rs_recv,
):
    row = lax.axis_index("row")
    col = lax.axis_index("col")
    z = lax.rem(col, NZ)
    yl = col // NZ
    core = lax.rem(row, 2)
    me16 = (row // 2) * 2 + yl
    me = core * HALF + me16

    zs = [z] + [lax.rem(z + k, NZ) for k in range(1, NZ)]
    x0, yh0 = row // 4, lax.rem(row // 2, 2)
    xs = [x0] + [lax.rem(x0 + k, 4) for k in range(1, 4)]
    yhs, yls, cores = (yh0, 1 - yh0), (yl, 1 - yl), (core, 1 - core)

    def slot_of(dx, dy, dl):
        return xs[dx] * 4 + yhs[dy] * 2 + yls[dl]

    def plane_id(dx, dy, dl, core_there):
        return {"row": xs[dx] * 4 + yhs[dy] * 2 + core_there, "col": yls[dl] * NZ + z}

    def z_id(direction):
        return {"row": row, "col": yl * NZ + zs[direction % NZ]}

    barrier = pltpu.get_barrier_semaphore()

    for dx, dy, dl in CHIPS:
        for dc in range(2):
            if (dx, dy, dl, dc) != (0, 0, 0, 0):
                there = plane_id(dx, dy, dl, cores[dc])
                pl.semaphore_signal(barrier, inc=1, device_id=there, device_id_type=MESH)
    for direction in (1, -1):
        pl.semaphore_signal(barrier, inc=1, device_id=z_id(direction), device_id_type=MESH)

    loads = [
        pltpu.make_async_copy(src, dst, in_sem.at[n])
        for n, (src, dst) in enumerate(
            ((left_hbm, left), (right_hbm, right), (out_hbm, pair_out), (cot_hbm, cot))
        )
    ]
    stores = [
        pltpu.make_async_copy(src, dst, out_sem.at[n])
        for n, (src, dst) in enumerate(
            (
                (result, result_hbm),
                (grad_out, grad_out_hbm),
                (grad_left, grad_left_hbm),
                (grad_right, grad_right_hbm),
            )
        )
    ]
    for load in loads:
        load.start()

    def remote(n, src, dst, there):
        return pltpu.make_async_remote_copy(
            src_ref=src, dst_ref=dst,
            send_sem=a2a_send.at[n], recv_sem=a2a_recv.at[n],
            device_id=there, device_id_type=MESH,
        )

    def all_start(n, src, dst, slot):
        pltpu.make_async_copy(src.at[me], dst.at[slot], a2a_recv.at[n]).start()

        for dx, dy, dl in CHIPS:
            for dc in range(2):
                if (dx, dy, dl, dc) != (0, 0, 0, 0):
                    p = cores[dc] * HALF + slot_of(dx, dy, dl)
                    remote(n, src.at[p], dst.at[slot], plane_id(dx, dy, dl, cores[dc])).start()

    def all_drain(n, src):
        part = src.at[pl.ds(0, PLANE - 1)]
        pltpu.make_async_copy(part, part, a2a_send.at[n]).wait()

    def part_start(n, kappa, src, dst):
        @pl.when(core == kappa)
        def _():
            pltpu.make_async_copy(src.at[me16], dst.at[me], a2a_recv.at[n]).start()

        @pl.when(core != kappa)
        def _():
            remote(n, src.at[me16], dst.at[me], plane_id(0, 0, 0, kappa)).start()

        for dx, dy, dl in CHIPS:
            if (dx, dy, dl) != (0, 0, 0):
                there = plane_id(dx, dy, dl, kappa)
                remote(n, src.at[slot_of(dx, dy, dl)], dst.at[me], there).start()

    def part_drain(n, kappa, src):
        @pl.when(core == kappa)
        def _():
            part = src.at[pl.ds(0, HALF - 1)]
            pltpu.make_async_copy(part, part, a2a_send.at[n]).wait()

        @pl.when(core != kappa)
        def _():
            pltpu.make_async_copy(src, src, a2a_send.at[n]).wait()

    def arrived(n, dst):
        pltpu.make_async_copy(dst, dst, a2a_recv.at[n]).wait()

    def z_slots(kappa, part):
        return pl.ds(HALF * kappa + QUART * part, QUART)

    def gather_copy(kappa, f, s):
        direction, part, _ = FLOWS[f]
        block = lbuf.at[zs[-direction * s % NZ], z_slots(kappa, part)]
        return pltpu.make_async_remote_copy(
            src_ref=block, dst_ref=block,
            send_sem=ag_send.at[kappa, f, s], recv_sem=ag_recv.at[kappa, f, s],
            device_id=z_id(direction), device_id_type=MESH,
        )

    def gather_start(kappa):
        for f in range(NF):
            gather_copy(kappa, f, 0).start()

    def gather_pump(kappa, s):
        for f in range(NF):
            if s < FLOWS[f][2]:
                gather_copy(kappa, f, s).wait_recv()
                if s + 1 < FLOWS[f][2]:
                    gather_copy(kappa, f, s + 1).start()

    def unmix_left(kappa, zz):
        for n in range(4):
            ylk, q = n // 2, n % 2
            x = [lbuf[zz, HALF * kappa + (4 * q + t) * 2 + ylk].astype(F32) for t in range(4)]
            y = exchange4(x)
            k0 = pl.multiple_of((ylk * NZ + zz) * 32, 32)
            lanes = pl.ds(256 * kappa + q * 128, 128)
            for h in range(HS):
                block = cat([y[b][8 * h : 8 * h + 8] for b in range(4)])
                lm[h, pl.ds(k0, 32), lanes] = block.astype(BF16)

    def unmix_gathered(kappa, s):
        if s < 3:
            unmix_left(kappa, zs[NZ - s - 1])
            unmix_left(kappa, zs[s + 1])
        else:
            unmix_left(kappa, zs[4])

    def unmix_pair(src, first, count, put):
        for m in range(count):
            y = swap64(src[first + 2 * m].astype(F32), src[first + 2 * m + 1].astype(F32))
            for h in range(HS):
                put(h, m, cat([y[g][16 * h : 16 * h + 16] for g in range(2)]).astype(BF16))

    def unmix_right():
        for kappa in range(2):

            def put(h, m, block):
                rm[h, pl.ds((2 * m + kappa) * 32, 32), :] = block

            unmix_pair(rbuf, HALF * kappa, 8, put)

    def unmix_d(kappa):
        def put(h, m, block):
            dm[h, pl.ds(256 * kappa + m * 32, 32), :] = block

        unmix_pair(dbuf, HALF * kappa, 8, put)

    def mix_pair(per_channel, blocks, put):
        for m in range(blocks):
            for h in range(HS):
                r0 = h * per_channel + m * 32
                y = swap64(scr[pl.ds(r0, 16), :], scr[pl.ds(r0 + 16, 16), :])
                for v in range(2):
                    put(m, v, h, y[v].astype(BF16))

    def triangle(kappa):
        for h in range(HS):
            scr[256 * h : 256 * h + 256, :] = dot_nn(rmt[h], lm[h, :, 256 * kappa : 256 * kappa + 256]).T

        def put(m, v, h, block):
            tsend[kappa, 2 * m + v, 16 * h : 16 * h + 16, :] = block

        mix_pair(256, 8, put)
        part_start(2 + kappa, kappa, tsend.at[kappa], tbuf)

    g_in, b_in, g_tri, b_tri = gain[...], bias[...], o_gain[...], o_bias[...]
    wg, wo = w_gate[...], w_out[...]

    def slab(kappa, n):
        @pl.when(core == kappa)
        def _():
            if n == 0:
                arrived(2 + kappa, tbuf)
                scr[...] = tbuf[...].reshape(2048, 128).astype(F32)
            slab_back(n, scr, scr2, up_s, tri_s)
            if n == 1:
                dsend[...] = scr2[...].astype(BF16).reshape(PLANE, 64, 128)
                all_start(4 + kappa, dsend, dbuf, me)

    def sum_copy(kappa, f, s):
        direction, part, steps = FLOWS[f]
        block = dls.at[zs[direction * (steps - s) % NZ], z_slots(kappa, part)]
        return pltpu.make_async_remote_copy(
            src_ref=block, dst_ref=rsbuf.at[kappa, f, s],
            send_sem=rs_send.at[kappa, f, s], recv_sem=rs_recv.at[kappa, f, s],
            device_id=z_id(direction), device_id_type=MESH,
        )

    def left_sums(kappa):
        arrived(4 + kappa, dbuf.at[pl.ds(HALF * kappa, HALF)])
        unmix_d(kappa)
        for h in range(HS):
            big[h] = dot_nt(rm[h], dm[h, 256 * kappa : 256 * kappa + 256, :])

        def pack(zz):
            for ylk in range(2):
                k0 = pl.multiple_of((ylk * NZ + zz) * 32, 32)
                for q in range(2):
                    x = [
                        cat([big[h, pl.ds(k0 + 8 * b, 8), 128 * q : 128 * q + 128] for h in range(HS)])
                        for b in range(4)
                    ]
                    y = exchange4(x)
                    for t in range(4):
                        dls[zz, HALF * kappa + (4 * q + t) * 2 + ylk] = y[t].astype(BF16)

        for k in (4, 3, 5):
            pack(zs[k])
        for f in range(NF):
            sum_copy(kappa, f, 0).start()
        for k in (2, 6, 1, 7, 0):
            pack(zs[k])

    def sum_pump(kappa, s):
        for f in range(NF):
            direction, part, steps = FLOWS[f]
            if s < steps:
                sum_copy(kappa, f, s).wait_recv()
                if s + 1 < steps:
                    here = (zs[direction * (steps - s - 1) % NZ], z_slots(kappa, part))
                    dls[here] = (dls[here].astype(F32) + rsbuf[kappa, f, s].astype(F32)).astype(BF16)
                    sum_copy(kappa, f, s + 1).start()

    def left_out(kappa):
        for part in range(4):
            total = dls[z, z_slots(kappa, part)].astype(F32)
            for f in range(NF):
                if FLOWS[f][1] == part:
                    total = total + rsbuf[kappa, f, FLOWS[f][2] - 1].astype(F32)
            dlsend[kappa, QUART * part : QUART * part + QUART] = total.astype(BF16)
        part_start(7 + kappa, kappa, dlsend.at[kappa], dlbuf)

    loads[0].wait()
    project_left(left, g_in, b_in, w_left[...], ls, lfac, scr)
    pl.semaphore_wait(barrier, PLANE - 1 + 2)
    all_start(0, ls, lbuf.at[z], me)
    loads[1].wait()
    project_right(right, g_in, b_in, w_right[...], rs, rfac, scr2)
    loads[2].wait()
    loads[3].wait()
    gate_rows(pair_out, cot, g_in, b_in, wg, wo, g_tri, gate_s, std_s, inv_s, up_s)
    arrived(0, lbuf.at[z])
    gather_start(0)
    all_start(1, rs, rbuf, me)
    unmix_left(0, z)
    unmix_left(1, z)
    gather_pump(0, 0)
    gather_start(1)
    unmix_gathered(0, 0)
    gather_pump(0, 1)
    gather_pump(1, 0)
    unmix_gathered(0, 1)
    unmix_gathered(1, 0)
    gather_pump(0, 2)
    gather_pump(1, 1)
    arrived(1, rbuf)
    unmix_right()
    for h in range(HS):
        rmt[h] = rm[h].T
    unmix_gathered(0, 2)
    gather_pump(0, 3)
    unmix_gathered(0, 3)

    triangle(0)
    gather_pump(1, 2)
    unmix_gathered(1, 1)
    unmix_gathered(1, 2)
    gather_pump(1, 3)
    unmix_gathered(1, 3)
    triangle(1)

    slab(0, 0)
    slab(0, 1)
    slab(1, 0)
    slab(1, 1)
    slab_rows(cot, g_in, g_tri, b_tri, wg, wo, gate_s, std_s, inv_s, tri_s, result, grad_out)
    stores[0].start()
    stores[1].start()
    left_sums(0)
    left_sums(1)
    sum_pump(0, 0)
    sum_pump(1, 0)
    for h in range(HS):
        scr[512 * h : 512 * h + 512, :] = dot_nn(lm[h], dm[h])

    def put_right(m, v, h, block):
        drsend[(m % 2) * HALF + (m // 2) * 2 + v, 16 * h : 16 * h + 16, :] = block

    mix_pair(512, 16, put_right)
    all_start(6, drsend, drbuf, me)
    sum_pump(0, 1)
    sum_pump(1, 1)
    prepare_left(left, lstd, linv)
    sum_pump(0, 2)
    sum_pump(1, 2)
    sum_pump(0, 3)
    left_out(0)
    sum_pump(1, 3)
    left_out(1)
    arrived(6, drbuf)
    scr[...] = drbuf[...].reshape(2048, 128).astype(F32)
    wr = w_right[...]
    back_right(0, right, rfac, g_in, wr, grad_right, scr)
    back_right(1, right, rfac, g_in, wr, grad_right, scr)
    stores[3].start()
    for kappa in range(2):

        @pl.when(core == kappa)
        def _():
            arrived(7 + kappa, dlbuf)

    scr[0:1024, :] = dlbuf[...].reshape(1024, 128).astype(F32)
    back_left(lstd, linv, lfac, g_in, w_left[...], grad_left, scr)
    stores[2].start()

    all_drain(0, ls)
    all_drain(1, rs)
    all_drain(6, drsend)
    for kappa in range(2):
        part_drain(2 + kappa, kappa, tsend.at[kappa])
        part_drain(7 + kappa, kappa, dlsend.at[kappa])

        @pl.when(core == kappa)
        def _():
            all_drain(4 + kappa, dsend)

        for f in range(NF):
            for s in range(FLOWS[f][2]):
                gather_copy(kappa, f, s).wait_send()
                sum_copy(kappa, f, s).wait_send()
    for store in stores:
        store.wait()


def hand_over_kernel(*refs):
    srcs, dsts, held = refs[:4], refs[4:8], refs[8:12]
    in_sem, out_sem = refs[12:]
    ins = [pltpu.make_async_copy(srcs[n], held[n], in_sem.at[n]) for n in range(4)]
    outs = [pltpu.make_async_copy(held[n], dsts[n], out_sem.at[n]) for n in range(4)]
    for copy in ins:
        copy.start()
    for n in range(4):
        ins[n].wait()
        outs[n].start()
    for copy in outs:
        copy.wait()


VMEM_LIMIT = 56 * 1024 * 1024


def per_device(
    pair_out, pair_left, pair_right, ln_gain, ln_bias, w_left, w_right, w_gate, w_out,
    out_gain, out_bias, cotangent,
):
    vm = pl.BlockSpec(memory_space=pltpu.VMEM)
    hbm = pl.BlockSpec(memory_space=pl.ANY)
    gain, bias = ln_gain.reshape(1, 128), ln_bias.reshape(1, 128)
    o_gain, o_bias = out_gain.reshape(1, 128), out_bias.reshape(1, 128)

    def vmem(*shape, dtype=BF16):
        return pltpu.VMEM(shape, dtype)

    def wide(*shape):
        return pltpu.VMEM(shape, F32)

    pair, lefts = (32, 48, 128), (32, 32, 128)
    slots, half_slots = vmem(PLANE, 64, 128), vmem(PLANE, 32, 128)
    dma = pltpu.SemaphoreType.DMA
    outs = tuple(jax.ShapeDtypeStruct(shape, BF16) for shape in (pair, pair, lefts, pair))
    made = pl.pallas_call(
        triangle_kernel,
        out_shape=outs,
        in_specs=[hbm] * 4 + [vm] * 8,
        out_specs=(hbm,) * 4,
        scratch_shapes=[
            vmem(*lefts), vmem(*pair), vmem(*pair), vmem(*pair),
            vmem(*pair), vmem(*pair), vmem(*lefts), vmem(*pair),
            half_slots, slots,
            wide(8, 256, 128), wide(16, 256, 128),
            wide(1536, 128), wide(1536, 128), wide(1536, 128),
            wide(1536, 128), wide(1536, 128), wide(1024, 128), wide(1024, 128),
            vmem(NZ, PLANE, 32, 128), slots,
            vmem(2, HALF, 64, 128), slots,
            slots, slots,
            slots, slots,
            vmem(NZ, PLANE, 32, 128), vmem(2, NF, 4, QUART, 32, 128),
            vmem(2, HALF, 32, 128), half_slots,
            vmem(HS, 512, 512), vmem(HS, 512, 128),
            vmem(HS, 128, 512), vmem(HS, 512, 128),
            wide(2048, 128), wide(2048, 128), wide(HS, 512, 256),
            dma((4,)), dma((4,)), dma((9,)), dma((9,)),
            dma((2, NF, 4)), dma((2, NF, 4)), dma((2, NF, 4)), dma((2, NF, 4)),
        ],
        compiler_params=pltpu.CompilerParams(
            vmem_limit_bytes=VMEM_LIMIT, collective_id=0, has_side_effects=True
        ),
        name="triangle",
    )(
        pair_left, pair_right, pair_out, cotangent, gain, bias, w_left, w_right, w_gate, w_out,
        o_gain, o_bias,
    )
    return pl.pallas_call(
        hand_over_kernel,
        out_shape=outs,
        in_specs=[hbm] * 4,
        out_specs=(hbm,) * 4,
        scratch_shapes=[vmem(*pair), vmem(*pair), vmem(*lefts), vmem(*pair), dma((4,)), dma((4,))],
        compiler_params=pltpu.CompilerParams(vmem_limit_bytes=VMEM_LIMIT),
        name="hand_over",
    )(*made)


def solution(mesh):
    pairs, lefts = P("row", "col", None), P("col", "row", None)
    return jax.shard_map(
        per_device,
        mesh=mesh,
        in_specs=(pairs, lefts, pairs, P(), P(), P(), P(), P(), P(), P(), P(), pairs),
        out_specs=(pairs, pairs, lefts, pairs),
        check_vma=False,
    )
```

```python
import jax
import jax.numpy as jnp
from jax import lax
from jax.experimental import pallas as pl
from jax.experimental.pallas import tpu as pltpu
from jax.sharding import PartitionSpec as P

MESH = pl.DeviceIdType.MESH
BF16 = jnp.bfloat16
F32 = jnp.float32
NZ = 8
PLANE = 32
HALF = PLANE // 2
HS = 4
EPS = 1e-05


def cat(parts, axis=0):
    return jnp.concatenate(parts, axis=axis)


def standardize(values):
    center = values - jnp.mean(values, axis=-1, keepdims=True)
    inverse = lax.rsqrt(jnp.mean(center * center, axis=-1, keepdims=True) + EPS)
    return center * inverse, inverse


def norm_back(upstream, standard, inverse, gain):
    scaled = upstream * gain
    return inverse * (
        scaled
        - jnp.mean(scaled, axis=-1, keepdims=True)
        - standard * jnp.mean(scaled * standard, axis=-1, keepdims=True)
    )


def dot_nn(a, b):
    return lax.dot_general(a, b, (((1,), (0,)), ((), ())), preferred_element_type=F32)


def dot_nt(a, b):
    return lax.dot_general(a, b, (((1,), (1,)), ((), ())), preferred_element_type=F32)


def swap64(x0, x1):
    low = lax.broadcasted_iota(jnp.int32, x0.shape, 1) < 64
    return (
        jnp.where(low, x0, pltpu.roll(x1, 64, 1)),
        jnp.where(low, pltpu.roll(x0, 64, 1), x1),
    )


def swap32(x0, x1):
    low = lax.broadcasted_iota(jnp.int32, x0.shape, 1) % 64 < 32
    return (
        jnp.where(low, x0, pltpu.roll(x1, 32, 1)),
        jnp.where(low, pltpu.roll(x0, 96, 1), x1),
    )


def exchange4(x):
    y0, y2 = swap64(x[0], x[2])
    y1, y3 = swap64(x[1], x[3])
    z0, z1 = swap32(y0, y1)
    z2, z3 = swap32(y2, y3)
    return z0, z1, z2, z3


def gate_of(pre):
    squash = jax.nn.sigmoid(pre[128:])
    gated = squash * pre[:128]
    return gated, cat([squash, gated * (1.0 - squash)])


def project_left(left, g, bi, w, ls, lfac, scr):
    x = cat([left[8 * b + a] for a in range(8) for b in range(4)]).astype(F32)
    standard, _ = standardize(x)
    pre = dot_nt(w.T, (standard * g + bi).astype(BF16))
    gated, factors = gate_of(pre)
    for a in range(8):
        lfac[a] = factors[:, 128 * a : 128 * a + 128]
        scr[pl.ds(a, 128, stride=8), :] = gated[:, 128 * a : 128 * a + 128]
    ls[...] = scr[0:1024, :].astype(BF16).reshape(PLANE, 32, 128)


def project_right(right, g, bi, w, rs, rfac, scr):
    zeros = jnp.zeros((16, 128), F32)
    wr = w.T

    def step(n, _):
        x = cat([right[16 * b + n * 8 + t] for t in range(8) for b in range(2)]).astype(F32)
        standard, _ = standardize(x)
        normed = standard * g + bi
        normed = cat([y for t in range(16) for y in (normed[48 * t : 48 * t + 48], zeros)])
        pre = dot_nt(wr, normed.astype(BF16))
        gated, factors = gate_of(pre)
        for t in range(8):
            rfac[n * 8 + t] = factors[:, 128 * t : 128 * t + 128]
            scr[pl.ds(n * 8 + t, 128, stride=16), :] = gated[:, 128 * t : 128 * t + 128]
        return 0

    lax.fori_loop(0, 2, step, 0)
    rs[...] = scr[...].astype(BF16).reshape(PLANE, 64, 128)


def gate_rows(pair_out, cot, g, bi, wg, wo, g_tri, gate_s, std_s, inv_s, up_s):
    def step(n, _):
        x = cat([pair_out[16 * b + n * 8 + t] for t in range(8) for b in range(2)]).astype(F32)
        standard, inverse = standardize(x)
        rows = pl.ds(pl.multiple_of(n * 768, 768), 768)
        gate = jax.nn.sigmoid(dot_nn((standard * g + bi).astype(BF16), wg))
        up = cat([cot[16 * b + n * 8 + t] for t in range(8) for b in range(2)]).astype(F32)
        scaled = dot_nt((up * gate).astype(BF16), wo) * g_tri
        up_s[rows, :] = scaled - jnp.mean(scaled, axis=-1, keepdims=True)
        gate_s[rows, :] = gate
        std_s[rows, :] = standard
        inv_s[rows, :] = jnp.broadcast_to(inverse, standard.shape)
        return 0

    lax.fori_loop(0, 2, step, 0)


def slab_back(n, scr, scr2, up_s, tri_s):
    zeros = jnp.zeros((16, 128), F32)
    parts = []
    for t in range(8):
        tri = scr[pl.ds(n * 8 + t, 128, stride=16), :].T
        parts += [tri[0:48], tri[64:112]]
    tri_std, tri_inv = standardize(cat(parts))
    rows = pl.ds(n * 768, 768)
    tri_s[rows, :] = tri_std
    up = up_s[rows, :]
    d_tri = tri_inv * (up - tri_std * jnp.mean(up * tri_std, axis=-1, keepdims=True))
    for t in range(8):
        o = 96 * t
        padded = cat([d_tri[o : o + 48], zeros, d_tri[o + 48 : o + 96], zeros])
        scr2[pl.ds(n * 8 + t, 128, stride=16), :] = padded.T


def slab_rows(cot, g_in, g_tri, b_tri, wg, wo, gate_s, std_s, inv_s, tri_s, result, grad_out):
    def step(n, _):
        rows = pl.ds(pl.multiple_of(n * 768, 768), 768)
        up = cat([cot[16 * b + n * 8 + t] for t in range(8) for b in range(2)]).astype(F32)
        gate = gate_s[rows, :]
        proj = dot_nn((tri_s[rows, :] * g_tri + b_tri).astype(BF16), wo)
        res = (gate * proj).astype(BF16)
        d_gate = (up * gate * proj * (1.0 - gate)).astype(BF16)
        g_out = norm_back(dot_nt(d_gate, wg), std_s[rows, :], inv_s[rows, :], g_in).astype(BF16)
        for t in range(8):
            for b in range(2):
                o = (2 * t + b) * 48
                result[16 * b + n * 8 + t] = res[o : o + 48]
                grad_out[16 * b + n * 8 + t] = g_out[o : o + 48]
        return 0

    lax.fori_loop(0, 2, step, 0)


def d_pre_of(d, factors):
    return cat([d * factors[:128], d * factors[128:]]).astype(BF16)


def prepare_left(left, lstd, linv):
    x = cat([left[8 * b + a] for a in range(8) for b in range(4)]).astype(F32)
    standard, inverse = standardize(x)
    lstd[...] = standard
    linv[...] = jnp.broadcast_to(inverse, standard.shape)


def back_left(lstd, linv, lfac, g, w, gl, scr):
    d = cat([scr[pl.ds(a, 128, stride=8), :] for a in range(8)], axis=1)
    factors = cat([lfac[a] for a in range(8)], axis=1)
    e = dot_nn(w, d_pre_of(d, factors)).T
    out = norm_back(e, lstd[...], linv[...], g).astype(BF16)
    for a in range(8):
        for b in range(4):
            o = 128 * a + 32 * b
            gl[8 * b + a] = out[o : o + 32]


def back_right(n, right, rfac, g, w, gr, scr):
    d = cat([scr[pl.ds(n * 8 + t, 128, stride=16), :] for t in range(8)], axis=1)
    factors = cat([rfac[n * 8 + t] for t in range(8)], axis=1)
    e = dot_nn(w, d_pre_of(d, factors)).T
    e = cat([y for t in range(8) for y in (e[128 * t : 128 * t + 48], e[128 * t + 64 : 128 * t + 112])])
    x = cat([right[16 * b + n * 8 + t] for t in range(8) for b in range(2)]).astype(F32)
    standard, inverse = standardize(x)
    out = norm_back(e, standard, inverse, g).astype(BF16)
    for t in range(8):
        for b in range(2):
            o = (2 * t + b) * 48
            gr[16 * b + n * 8 + t] = out[o : o + 48]


FLOWS = tuple(
    (direction, part, 4 if (part < 2) == (direction > 0) else 3)
    for part in range(4)
    for direction in (1, -1)
)
NF = len(FLOWS)
CHIPS = tuple((dx, dy, dl) for dx in (2, 1, 3, 0) for dy in (1, 0) for dl in (1, 0))
QUART = HALF // 4


def triangle_kernel(
    left_hbm, right_hbm, out_hbm, cot_hbm, *rest
):
    small_hbm, outs_hbm, small, rest = rest[:8], rest[8:12], rest[12:20], rest[20:]
    result_hbm, grad_out_hbm, grad_left_hbm, grad_right_hbm = outs_hbm
    gain, bias, w_left, w_right, w_gate, w_out, o_gain, o_bias = small
    (
        left, right, pair_out, cot, result, grad_out, grad_left, grad_right,
        ls, rs, lfac, rfac, gate_s, std_s, inv_s, up_s, tri_s, lstd, linv,
        lbuf, rbuf, tsend, tbuf, dsend, dbuf, drsend, drbuf, dls, rsbuf, dlsend, dlbuf,
        lm, rm, rmt, dm, scr, scr2, big,
        small_sem, in_sem, out_sem, a2a_send, a2a_recv, ag_send, ag_recv, rs_send, rs_recv,
    ) = rest
    row = lax.axis_index("row")
    col = lax.axis_index("col")
    z = lax.rem(col, NZ)
    yl = col // NZ
    core = lax.rem(row, 2)
    me16 = (row // 2) * 2 + yl
    me = core * HALF + me16

    zs = [z] + [lax.rem(z + k, NZ) for k in range(1, NZ)]
    x0, yh0 = row // 4, lax.rem(row // 2, 2)
    xs = [x0] + [lax.rem(x0 + k, 4) for k in range(1, 4)]
    yhs, yls, cores = (yh0, 1 - yh0), (yl, 1 - yl), (core, 1 - core)

    def slot_of(dx, dy, dl):
        return xs[dx] * 4 + yhs[dy] * 2 + yls[dl]

    def plane_id(dx, dy, dl, core_there):
        return {"row": xs[dx] * 4 + yhs[dy] * 2 + core_there, "col": yls[dl] * NZ + z}

    def z_id(direction):
        return {"row": row, "col": yl * NZ + zs[direction % NZ]}

    barrier = pltpu.get_barrier_semaphore()

    for dx, dy, dl in CHIPS:
        for dc in range(2):
            if (dx, dy, dl, dc) != (0, 0, 0, 0):
                there = plane_id(dx, dy, dl, cores[dc])
                pl.semaphore_signal(barrier, inc=1, device_id=there, device_id_type=MESH)
    for direction in (1, -1):
        pl.semaphore_signal(barrier, inc=1, device_id=z_id(direction), device_id_type=MESH)

    loads = [
        pltpu.make_async_copy(src, dst, in_sem.at[n])
        for n, (src, dst) in enumerate(
            ((left_hbm, left), (right_hbm, right), (out_hbm, pair_out), (cot_hbm, cot))
        )
    ]
    stores = [
        pltpu.make_async_copy(src, dst, out_sem.at[n])
        for n, (src, dst) in enumerate(
            (
                (result, result_hbm),
                (grad_out, grad_out_hbm),
                (grad_left, grad_left_hbm),
                (grad_right, grad_right_hbm),
            )
        )
    ]
    small_loads = [
        pltpu.make_async_copy(small_hbm[n], small[n], small_sem.at[n]) for n in range(8)
    ]
    loads[0].start()
    for load in small_loads:
        load.start()
    for load in loads[1:]:
        load.start()

    def remote(n, src, dst, there):
        return pltpu.make_async_remote_copy(
            src_ref=src, dst_ref=dst,
            send_sem=a2a_send.at[n], recv_sem=a2a_recv.at[n],
            device_id=there, device_id_type=MESH,
        )

    def all_start(n, src, dst, slot):
        pltpu.make_async_copy(src.at[me], dst.at[slot], a2a_recv.at[n]).start()

        for dx, dy, dl in CHIPS:
            for dc in range(2):
                if (dx, dy, dl, dc) != (0, 0, 0, 0):
                    p = cores[dc] * HALF + slot_of(dx, dy, dl)
                    remote(n, src.at[p], dst.at[slot], plane_id(dx, dy, dl, cores[dc])).start()

    def all_drain(n, src):
        part = src.at[pl.ds(0, PLANE - 1)]
        pltpu.make_async_copy(part, part, a2a_send.at[n]).wait()

    def part_start(n, kappa, src, dst):
        @pl.when(core == kappa)
        def _():
            pltpu.make_async_copy(src.at[me16], dst.at[me], a2a_recv.at[n]).start()

        @pl.when(core != kappa)
        def _():
            remote(n, src.at[me16], dst.at[me], plane_id(0, 0, 0, kappa)).start()

        for dx, dy, dl in CHIPS:
            if (dx, dy, dl) != (0, 0, 0):
                there = plane_id(dx, dy, dl, kappa)
                remote(n, src.at[slot_of(dx, dy, dl)], dst.at[me], there).start()

    def part_drain(n, kappa, src):
        @pl.when(core == kappa)
        def _():
            part = src.at[pl.ds(0, HALF - 1)]
            pltpu.make_async_copy(part, part, a2a_send.at[n]).wait()

        @pl.when(core != kappa)
        def _():
            pltpu.make_async_copy(src, src, a2a_send.at[n]).wait()

    def arrived(n, dst):
        pltpu.make_async_copy(dst, dst, a2a_recv.at[n]).wait()

    def z_slots(kappa, part):
        return pl.ds(HALF * kappa + QUART * part, QUART)

    def gather_copy(kappa, f, s):
        direction, part, _ = FLOWS[f]
        block = lbuf.at[zs[-direction * s % NZ], z_slots(kappa, part)]
        return pltpu.make_async_remote_copy(
            src_ref=block, dst_ref=block,
            send_sem=ag_send.at[kappa, f, s], recv_sem=ag_recv.at[kappa, f, s],
            device_id=z_id(direction), device_id_type=MESH,
        )

    def gather_start(kappa):
        for f in range(NF):
            gather_copy(kappa, f, 0).start()

    def gather_pump(kappa, s):
        for f in range(NF):
            if s < FLOWS[f][2]:
                gather_copy(kappa, f, s).wait_recv()
                if s + 1 < FLOWS[f][2]:
                    gather_copy(kappa, f, s + 1).start()

    def unmix_left(kappa, zz):
        for n in range(4):
            ylk, q = n // 2, n % 2
            x = [lbuf[zz, HALF * kappa + (4 * q + t) * 2 + ylk].astype(F32) for t in range(4)]
            y = exchange4(x)
            k0 = pl.multiple_of((ylk * NZ + zz) * 32, 32)
            lanes = pl.ds(256 * kappa + q * 128, 128)
            for h in range(HS):
                block = cat([y[b][8 * h : 8 * h + 8] for b in range(4)])
                lm[h, pl.ds(k0, 32), lanes] = block.astype(BF16)

    def unmix_gathered(kappa, s):
        if s < 3:
            unmix_left(kappa, zs[NZ - s - 1])
            unmix_left(kappa, zs[s + 1])
        else:
            unmix_left(kappa, zs[4])

    def unmix_pair(src, first, count, put):
        for m in range(count):
            y = swap64(src[first + 2 * m].astype(F32), src[first + 2 * m + 1].astype(F32))
            for h in range(HS):
                put(h, m, cat([y[g][16 * h : 16 * h + 16] for g in range(2)]).astype(BF16))

    def unmix_right():
        for kappa in range(2):

            def put(h, m, block):
                rm[h, pl.ds((2 * m + kappa) * 32, 32), :] = block

            unmix_pair(rbuf, HALF * kappa, 8, put)

    def unmix_d(kappa):
        def put(h, m, block):
            dm[h, pl.ds(256 * kappa + m * 32, 32), :] = block

        unmix_pair(dbuf, HALF * kappa, 8, put)

    def mix_pair(per_channel, blocks, put):
        for m in range(blocks):
            for h in range(HS):
                r0 = h * per_channel + m * 32
                y = swap64(scr[pl.ds(r0, 16), :], scr[pl.ds(r0 + 16, 16), :])
                for v in range(2):
                    put(m, v, h, y[v].astype(BF16))

    def triangle(kappa):
        for h in range(HS):
            scr[256 * h : 256 * h + 256, :] = dot_nn(rmt[h], lm[h, :, 256 * kappa : 256 * kappa + 256]).T

        def put(m, v, h, block):
            tsend[kappa, 2 * m + v, 16 * h : 16 * h + 16, :] = block

        mix_pair(256, 8, put)
        part_start(2 + kappa, kappa, tsend.at[kappa], tbuf)

    for load in small_loads:
        load.wait()
    g_in, b_in, g_tri, b_tri = gain[...], bias[...], o_gain[...], o_bias[...]
    wg, wo = w_gate[...], w_out[...]

    def slab(kappa, n):
        @pl.when(core == kappa)
        def _():
            if n == 0:
                arrived(2 + kappa, tbuf)
                scr[...] = tbuf[...].reshape(2048, 128).astype(F32)
            slab_back(n, scr, scr2, up_s, tri_s)
            if n == 1:
                dsend[...] = scr2[...].astype(BF16).reshape(PLANE, 64, 128)
                all_start(4 + kappa, dsend, dbuf, me)

    def sum_copy(kappa, f, s):
        direction, part, steps = FLOWS[f]
        block = dls.at[zs[direction * (steps - s) % NZ], z_slots(kappa, part)]
        return pltpu.make_async_remote_copy(
            src_ref=block, dst_ref=rsbuf.at[kappa, f, s],
            send_sem=rs_send.at[kappa, f, s], recv_sem=rs_recv.at[kappa, f, s],
            device_id=z_id(direction), device_id_type=MESH,
        )

    def left_sums(kappa):
        arrived(4 + kappa, dbuf.at[pl.ds(HALF * kappa, HALF)])
        unmix_d(kappa)
        for h in range(HS):
            big[h] = dot_nt(rm[h], dm[h, 256 * kappa : 256 * kappa + 256, :])

        def pack(zz):
            for ylk in range(2):
                k0 = pl.multiple_of((ylk * NZ + zz) * 32, 32)
                for q in range(2):
                    x = [
                        cat([big[h, pl.ds(k0 + 8 * b, 8), 128 * q : 128 * q + 128] for h in range(HS)])
                        for b in range(4)
                    ]
                    y = exchange4(x)
                    for t in range(4):
                        dls[zz, HALF * kappa + (4 * q + t) * 2 + ylk] = y[t].astype(BF16)

        for k in (4, 3, 5):
            pack(zs[k])
            for f in range(NF):
                direction, _, steps = FLOWS[f]
                if direction * steps % NZ == k:
                    sum_copy(kappa, f, 0).start()
        for k in (2, 6, 1, 7, 0):
            pack(zs[k])

    def sum_pump(kappa, s):
        for f in range(NF):
            direction, part, steps = FLOWS[f]
            if s < steps:
                sum_copy(kappa, f, s).wait_recv()
                if s + 1 < steps:
                    here = (zs[direction * (steps - s - 1) % NZ], z_slots(kappa, part))
                    dls[here] = (dls[here].astype(F32) + rsbuf[kappa, f, s].astype(F32)).astype(BF16)
                    sum_copy(kappa, f, s + 1).start()

    def left_out(kappa):
        for part in range(4):
            total = dls[z, z_slots(kappa, part)].astype(F32)
            for f in range(NF):
                if FLOWS[f][1] == part:
                    total = total + rsbuf[kappa, f, FLOWS[f][2] - 1].astype(F32)
            dlsend[kappa, QUART * part : QUART * part + QUART] = total.astype(BF16)
        part_start(7 + kappa, kappa, dlsend.at[kappa], dlbuf)

    loads[0].wait()
    project_left(left, g_in, b_in, w_left[...], ls, lfac, scr)
    pl.semaphore_wait(barrier, PLANE - 1 + 2)
    all_start(0, ls, lbuf.at[z], me)
    loads[1].wait()
    project_right(right, g_in, b_in, w_right[...], rs, rfac, scr2)
    loads[2].wait()
    loads[3].wait()
    gate_rows(pair_out, cot, g_in, b_in, wg, wo, g_tri, gate_s, std_s, inv_s, up_s)
    arrived(0, lbuf.at[z])
    gather_start(0)
    all_start(1, rs, rbuf, me)
    unmix_left(0, z)
    unmix_left(1, z)
    gather_pump(0, 0)
    gather_start(1)
    unmix_gathered(0, 0)
    gather_pump(0, 1)
    gather_pump(1, 0)
    unmix_gathered(0, 1)
    unmix_gathered(1, 0)
    gather_pump(0, 2)
    gather_pump(1, 1)
    arrived(1, rbuf)
    unmix_right()
    for h in range(HS):
        rmt[h] = rm[h].T
    unmix_gathered(0, 2)
    gather_pump(0, 3)
    unmix_gathered(0, 3)

    triangle(0)
    gather_pump(1, 2)
    unmix_gathered(1, 1)
    unmix_gathered(1, 2)
    gather_pump(1, 3)
    unmix_gathered(1, 3)
    triangle(1)

    slab(0, 0)
    slab(0, 1)
    slab(1, 0)
    slab(1, 1)
    left_sums(0)
    left_sums(1)
    sum_pump(0, 0)
    sum_pump(1, 0)
    for h in range(HS):
        scr[512 * h : 512 * h + 512, :] = dot_nn(lm[h], dm[h])

    def put_right(m, v, h, block):
        drsend[(m % 2) * HALF + (m // 2) * 2 + v, 16 * h : 16 * h + 16, :] = block

    mix_pair(512, 16, put_right)
    all_start(6, drsend, drbuf, me)
    sum_pump(0, 1)
    sum_pump(1, 1)
    slab_rows(cot, g_in, g_tri, b_tri, wg, wo, gate_s, std_s, inv_s, tri_s, result, grad_out)
    stores[0].start()
    stores[1].start()
    prepare_left(left, lstd, linv)
    sum_pump(0, 2)
    sum_pump(1, 2)
    sum_pump(0, 3)
    left_out(0)
    sum_pump(1, 3)
    left_out(1)
    arrived(6, drbuf)
    scr[...] = drbuf[...].reshape(2048, 128).astype(F32)
    wr = w_right[...]
    back_right(0, right, rfac, g_in, wr, grad_right, scr)
    back_right(1, right, rfac, g_in, wr, grad_right, scr)
    stores[3].start()
    for kappa in range(2):

        @pl.when(core == kappa)
        def _():
            arrived(7 + kappa, dlbuf)

    scr[0:1024, :] = dlbuf[...].reshape(1024, 128).astype(F32)
    back_left(lstd, linv, lfac, g_in, w_left[...], grad_left, scr)
    stores[2].start()

    all_drain(0, ls)
    all_drain(1, rs)
    all_drain(6, drsend)
    for kappa in range(2):
        part_drain(2 + kappa, kappa, tsend.at[kappa])
        part_drain(7 + kappa, kappa, dlsend.at[kappa])

        @pl.when(core == kappa)
        def _():
            all_drain(4 + kappa, dsend)

        for f in range(NF):
            for s in range(FLOWS[f][2]):
                gather_copy(kappa, f, s).wait_send()
                sum_copy(kappa, f, s).wait_send()
    for store in stores:
        store.wait()


def hand_over_kernel(*refs):
    srcs, dsts, held = refs[:4], refs[4:8], refs[8:12]
    in_sem, out_sem = refs[12:]
    pieces = [(n, p) for p in range(2) for n in range(4)]

    def copy(froms, tos, sems, n, p):
        rows = pl.ds(16 * p, 16)
        return pltpu.make_async_copy(froms[n].at[rows], tos[n].at[rows], sems.at[n, p])

    for n, p in pieces:
        copy(srcs, held, in_sem, n, p).start()
    for n, p in pieces:
        copy(srcs, held, in_sem, n, p).wait()
        copy(held, dsts, out_sem, n, p).start()
    for n, p in pieces:
        copy(held, dsts, out_sem, n, p).wait()


VMEM_LIMIT = 56 * 1024 * 1024


def per_device(
    pair_out, pair_left, pair_right, ln_gain, ln_bias, w_left, w_right, w_gate, w_out,
    out_gain, out_bias, cotangent,
):
    hbm = pl.BlockSpec(memory_space=pl.ANY)
    gain, bias = ln_gain.reshape(1, 128), ln_bias.reshape(1, 128)
    o_gain, o_bias = out_gain.reshape(1, 128), out_bias.reshape(1, 128)

    def vmem(*shape, dtype=BF16):
        return pltpu.VMEM(shape, dtype)

    def wide(*shape):
        return pltpu.VMEM(shape, F32)

    pair, lefts = (32, 48, 128), (32, 32, 128)
    small = [wide(1, 128), wide(1, 128), vmem(128, 256), vmem(128, 256)]
    small += [vmem(128, 128), vmem(128, 128), wide(1, 128), wide(1, 128)]
    slots, half_slots = vmem(PLANE, 64, 128), vmem(PLANE, 32, 128)
    dma = pltpu.SemaphoreType.DMA
    outs = tuple(jax.ShapeDtypeStruct(shape, BF16) for shape in (pair, pair, lefts, pair))
    made = pl.pallas_call(
        triangle_kernel,
        out_shape=outs,
        in_specs=[hbm] * 12,
        out_specs=(hbm,) * 4,
        scratch_shapes=small + [
            vmem(*lefts), vmem(*pair), vmem(*pair), vmem(*pair),
            vmem(*pair), vmem(*pair), vmem(*lefts), vmem(*pair),
            half_slots, slots,
            wide(8, 256, 128), wide(16, 256, 128),
            wide(1536, 128), wide(1536, 128), wide(1536, 128),
            wide(1536, 128), wide(1536, 128), wide(1024, 128), wide(1024, 128),
            vmem(NZ, PLANE, 32, 128), slots,
            vmem(2, HALF, 64, 128), slots,
            slots, slots,
            slots, slots,
            vmem(NZ, PLANE, 32, 128), vmem(2, NF, 4, QUART, 32, 128),
            vmem(2, HALF, 32, 128), half_slots,
            vmem(HS, 512, 512), vmem(HS, 512, 128),
            vmem(HS, 128, 512), vmem(HS, 512, 128),
            wide(2048, 128), wide(2048, 128), wide(HS, 512, 256),
            dma((8,)), dma((4,)), dma((4,)), dma((9,)), dma((9,)),
            dma((2, NF, 4)), dma((2, NF, 4)), dma((2, NF, 4)), dma((2, NF, 4)),
        ],
        compiler_params=pltpu.CompilerParams(
            vmem_limit_bytes=VMEM_LIMIT, collective_id=0, has_side_effects=True
        ),
        name="triangle",
    )(
        pair_left, pair_right, pair_out, cotangent, gain, bias, w_left, w_right, w_gate, w_out,
        o_gain, o_bias,
    )
    return pl.pallas_call(
        hand_over_kernel,
        out_shape=outs,
        in_specs=[hbm] * 4,
        out_specs=(hbm,) * 4,
        scratch_shapes=[vmem(*pair), vmem(*pair), vmem(*lefts), vmem(*pair), dma((4, 2)), dma((4, 2))],
        compiler_params=pltpu.CompilerParams(vmem_limit_bytes=VMEM_LIMIT),
        name="hand_over",
    )(*made)


def solution(mesh):
    pairs, lefts = P("row", "col", None), P("col", "row", None)
    return jax.shard_map(
        per_device,
        mesh=mesh,
        in_specs=(pairs, lefts, pairs, P(), P(), P(), P(), P(), P(), P(), P(), pairs),
        out_specs=(pairs, pairs, lefts, pairs),
        check_vma=False,
    )
```

```python
import jax
import jax.numpy as jnp
from jax import lax
from jax.experimental import pallas as pl
from jax.experimental.pallas import tpu as pltpu
from jax.sharding import PartitionSpec as P

MESH = pl.DeviceIdType.MESH
BF16 = jnp.bfloat16
F32 = jnp.float32
NZ = 8
PLANE = 32
HALF = PLANE // 2
HS = 4
EPS = 1e-05


def cat(parts, axis=0):
    return jnp.concatenate(parts, axis=axis)


def standardize(values):
    center = values - jnp.mean(values, axis=-1, keepdims=True)
    inverse = lax.rsqrt(jnp.mean(center * center, axis=-1, keepdims=True) + EPS)
    return center * inverse, inverse


def norm_back(upstream, standard, inverse, gain):
    scaled = upstream * gain
    return inverse * (
        scaled
        - jnp.mean(scaled, axis=-1, keepdims=True)
        - standard * jnp.mean(scaled * standard, axis=-1, keepdims=True)
    )


def dot_nn(a, b):
    return lax.dot_general(a, b, (((1,), (0,)), ((), ())), preferred_element_type=F32)


def dot_nt(a, b):
    return lax.dot_general(a, b, (((1,), (1,)), ((), ())), preferred_element_type=F32)


def swap64(x0, x1):
    low = lax.broadcasted_iota(jnp.int32, x0.shape, 1) < 64
    return (
        jnp.where(low, x0, pltpu.roll(x1, 64, 1)),
        jnp.where(low, pltpu.roll(x0, 64, 1), x1),
    )


def swap32(x0, x1):
    low = lax.broadcasted_iota(jnp.int32, x0.shape, 1) % 64 < 32
    return (
        jnp.where(low, x0, pltpu.roll(x1, 32, 1)),
        jnp.where(low, pltpu.roll(x0, 96, 1), x1),
    )


def exchange4(x):
    y0, y2 = swap64(x[0], x[2])
    y1, y3 = swap64(x[1], x[3])
    z0, z1 = swap32(y0, y1)
    z2, z3 = swap32(y2, y3)
    return z0, z1, z2, z3


def gate_of(pre):
    squash = jax.nn.sigmoid(pre[128:])
    gated = squash * pre[:128]
    return gated, cat([squash, gated * (1.0 - squash)])


def project_left(left, g, bi, w, ls, lfac, scr):
    x = cat([left[8 * b + a] for a in range(8) for b in range(4)]).astype(F32)
    standard, _ = standardize(x)
    pre = dot_nt(w.T, (standard * g + bi).astype(BF16))
    gated, factors = gate_of(pre)
    for a in range(8):
        lfac[a] = factors[:, 128 * a : 128 * a + 128]
        scr[pl.ds(a, 128, stride=8), :] = gated[:, 128 * a : 128 * a + 128]
    ls[...] = scr[0:1024, :].astype(BF16).reshape(PLANE, 32, 128)


def project_right(right, g, bi, w, rs, rfac, scr):
    zeros = jnp.zeros((16, 128), F32)
    wr = w.T

    def step(n, _):
        x = cat([right[16 * b + n * 8 + t] for t in range(8) for b in range(2)]).astype(F32)
        standard, _ = standardize(x)
        normed = standard * g + bi
        normed = cat([y for t in range(16) for y in (normed[48 * t : 48 * t + 48], zeros)])
        pre = dot_nt(wr, normed.astype(BF16))
        gated, factors = gate_of(pre)
        for t in range(8):
            rfac[n * 8 + t] = factors[:, 128 * t : 128 * t + 128]
            scr[pl.ds(n * 8 + t, 128, stride=16), :] = gated[:, 128 * t : 128 * t + 128]
        return 0

    lax.fori_loop(0, 2, step, 0)
    rs[...] = scr[...].astype(BF16).reshape(PLANE, 64, 128)


def gate_rows(pair_out, cot, g, bi, wg, wo, g_tri, gate_s, std_s, inv_s, up_s):
    def step(n, _):
        x = cat([pair_out[16 * b + n * 8 + t] for t in range(8) for b in range(2)]).astype(F32)
        standard, inverse = standardize(x)
        rows = pl.ds(pl.multiple_of(n * 768, 768), 768)
        gate = jax.nn.sigmoid(dot_nn((standard * g + bi).astype(BF16), wg))
        up = cat([cot[16 * b + n * 8 + t] for t in range(8) for b in range(2)]).astype(F32)
        scaled = dot_nt((up * gate).astype(BF16), wo) * g_tri
        up_s[rows, :] = scaled - jnp.mean(scaled, axis=-1, keepdims=True)
        gate_s[rows, :] = gate
        std_s[rows, :] = standard
        inv_s[rows, :] = jnp.broadcast_to(inverse, standard.shape)
        return 0

    lax.fori_loop(0, 2, step, 0)


def slab_back(n, scr, scr2, up_s, tri_s):
    zeros = jnp.zeros((16, 128), F32)
    parts = []
    for t in range(8):
        tri = scr[pl.ds(n * 8 + t, 128, stride=16), :].T
        parts += [tri[0:48], tri[64:112]]
    tri_std, tri_inv = standardize(cat(parts))
    rows = pl.ds(n * 768, 768)
    tri_s[rows, :] = tri_std
    up = up_s[rows, :]
    d_tri = tri_inv * (up - tri_std * jnp.mean(up * tri_std, axis=-1, keepdims=True))
    for t in range(8):
        o = 96 * t
        padded = cat([d_tri[o : o + 48], zeros, d_tri[o + 48 : o + 96], zeros])
        scr2[pl.ds(n * 8 + t, 128, stride=16), :] = padded.T


def slab_rows(cot, g_in, g_tri, b_tri, wg, wo, gate_s, std_s, inv_s, tri_s, result, grad_out):
    def step(n, _):
        rows = pl.ds(pl.multiple_of(n * 768, 768), 768)
        up = cat([cot[16 * b + n * 8 + t] for t in range(8) for b in range(2)]).astype(F32)
        gate = gate_s[rows, :]
        proj = dot_nn((tri_s[rows, :] * g_tri + b_tri).astype(BF16), wo)
        res = (gate * proj).astype(BF16)
        d_gate = (up * gate * proj * (1.0 - gate)).astype(BF16)
        g_out = norm_back(dot_nt(d_gate, wg), std_s[rows, :], inv_s[rows, :], g_in).astype(BF16)
        for t in range(8):
            for b in range(2):
                o = (2 * t + b) * 48
                result[16 * b + n * 8 + t] = res[o : o + 48]
                grad_out[16 * b + n * 8 + t] = g_out[o : o + 48]
        return 0

    lax.fori_loop(0, 2, step, 0)


def d_pre_of(d, factors):
    return cat([d * factors[:128], d * factors[128:]]).astype(BF16)


def prepare_left(left, lstd, linv):
    x = cat([left[8 * b + a] for a in range(8) for b in range(4)]).astype(F32)
    standard, inverse = standardize(x)
    lstd[...] = standard
    linv[...] = jnp.broadcast_to(inverse, standard.shape)


def back_left(lstd, linv, lfac, g, w, gl, scr):
    d = cat([scr[pl.ds(a, 128, stride=8), :] for a in range(8)], axis=1)
    factors = cat([lfac[a] for a in range(8)], axis=1)
    e = dot_nn(w, d_pre_of(d, factors)).T
    out = norm_back(e, lstd[...], linv[...], g).astype(BF16)
    for a in range(8):
        for b in range(4):
            o = 128 * a + 32 * b
            gl[8 * b + a] = out[o : o + 32]


def back_right(n, right, rfac, g, w, gr, scr):
    d = cat([scr[pl.ds(n * 8 + t, 128, stride=16), :] for t in range(8)], axis=1)
    factors = cat([rfac[n * 8 + t] for t in range(8)], axis=1)
    e = dot_nn(w, d_pre_of(d, factors)).T
    e = cat([y for t in range(8) for y in (e[128 * t : 128 * t + 48], e[128 * t + 64 : 128 * t + 112])])
    x = cat([right[16 * b + n * 8 + t] for t in range(8) for b in range(2)]).astype(F32)
    standard, inverse = standardize(x)
    out = norm_back(e, standard, inverse, g).astype(BF16)
    for t in range(8):
        for b in range(2):
            o = (2 * t + b) * 48
            gr[16 * b + n * 8 + t] = out[o : o + 48]


FLOWS = tuple(
    (direction, part, 4 if (part < 2) == (direction > 0) else 3)
    for part in range(4)
    for direction in (1, -1)
)
NF = len(FLOWS)
CHIPS = tuple((dx, dy, dl) for dx in (2, 1, 3, 0) for dy in (1, 0) for dl in (1, 0))
QUART = HALF // 4


def triangle_kernel(
    left_hbm, right_hbm, out_hbm, cot_hbm, *rest
):
    small_hbm, outs_hbm, small, rest = rest[:8], rest[8:12], rest[12:20], rest[20:]
    result_hbm, grad_out_hbm, grad_left_hbm, grad_right_hbm = outs_hbm
    gain, bias, w_left, w_right, w_gate, w_out, o_gain, o_bias = small
    (
        left, right, pair_out, cot, result, grad_out, grad_left, grad_right,
        ls, rs, lfac, rfac, gate_s, std_s, inv_s, up_s, tri_s, lstd, linv,
        lbuf, rbuf, tsend, tbuf, dsend, dbuf, drsend, drbuf, dls, rsbuf, dlsend, dlbuf,
        lm, rm, rmt, dm, scr, scr2, big,
        small_sem, in_sem, out_sem, a2a_send, a2a_recv, ag_send, ag_recv, rs_send, rs_recv,
    ) = rest
    row = lax.axis_index("row")
    col = lax.axis_index("col")
    z = lax.rem(col, NZ)
    yl = col // NZ
    core = lax.rem(row, 2)
    me16 = (row // 2) * 2 + yl
    me = core * HALF + me16

    zs = [z] + [lax.rem(z + k, NZ) for k in range(1, NZ)]
    x0, yh0 = row // 4, lax.rem(row // 2, 2)
    xs = [x0] + [lax.rem(x0 + k, 4) for k in range(1, 4)]
    yhs, yls, cores = (yh0, 1 - yh0), (yl, 1 - yl), (core, 1 - core)

    def slot_of(dx, dy, dl):
        return xs[dx] * 4 + yhs[dy] * 2 + yls[dl]

    def plane_id(dx, dy, dl, core_there):
        return {"row": xs[dx] * 4 + yhs[dy] * 2 + core_there, "col": yls[dl] * NZ + z}

    def z_id(direction):
        return {"row": row, "col": yl * NZ + zs[direction % NZ]}

    barrier = pltpu.get_barrier_semaphore()

    for dx, dy, dl in CHIPS:
        for dc in range(2):
            if (dx, dy, dl, dc) != (0, 0, 0, 0):
                there = plane_id(dx, dy, dl, cores[dc])
                pl.semaphore_signal(barrier, inc=1, device_id=there, device_id_type=MESH)
    for direction in (1, -1):
        pl.semaphore_signal(barrier, inc=1, device_id=z_id(direction), device_id_type=MESH)

    loads = [
        pltpu.make_async_copy(src, dst, in_sem.at[n])
        for n, (src, dst) in enumerate(
            ((left_hbm, left), (right_hbm, right), (out_hbm, pair_out), (cot_hbm, cot))
        )
    ]
    stores = [
        pltpu.make_async_copy(src, dst, out_sem.at[n])
        for n, (src, dst) in enumerate(
            (
                (result, result_hbm),
                (grad_out, grad_out_hbm),
                (grad_left, grad_left_hbm),
                (grad_right, grad_right_hbm),
            )
        )
    ]
    small_loads = [
        pltpu.make_async_copy(small_hbm[n], small[n], small_sem.at[n]) for n in range(8)
    ]
    loads[0].start()
    for load in small_loads:
        load.start()
    for load in loads[1:]:
        load.start()

    def remote(n, src, dst, there):
        return pltpu.make_async_remote_copy(
            src_ref=src, dst_ref=dst,
            send_sem=a2a_send.at[n], recv_sem=a2a_recv.at[n],
            device_id=there, device_id_type=MESH,
        )

    def all_start(n, src, dst, slot):
        pltpu.make_async_copy(src.at[me], dst.at[slot], a2a_recv.at[n]).start()

        for dx, dy, dl in CHIPS:
            for dc in range(2):
                if (dx, dy, dl, dc) != (0, 0, 0, 0):
                    p = cores[dc] * HALF + slot_of(dx, dy, dl)
                    remote(n, src.at[p], dst.at[slot], plane_id(dx, dy, dl, cores[dc])).start()

    def all_drain(n, src):
        part = src.at[pl.ds(0, PLANE - 1)]
        pltpu.make_async_copy(part, part, a2a_send.at[n]).wait()

    def part_start(n, kappa, src, dst):
        @pl.when(core == kappa)
        def _():
            pltpu.make_async_copy(src.at[me16], dst.at[me], a2a_recv.at[n]).start()

        @pl.when(core != kappa)
        def _():
            remote(n, src.at[me16], dst.at[me], plane_id(0, 0, 0, kappa)).start()

        for dx, dy, dl in CHIPS:
            if (dx, dy, dl) != (0, 0, 0):
                there = plane_id(dx, dy, dl, kappa)
                remote(n, src.at[slot_of(dx, dy, dl)], dst.at[me], there).start()

    def part_drain(n, kappa, src):
        @pl.when(core == kappa)
        def _():
            part = src.at[pl.ds(0, HALF - 1)]
            pltpu.make_async_copy(part, part, a2a_send.at[n]).wait()

        @pl.when(core != kappa)
        def _():
            pltpu.make_async_copy(src, src, a2a_send.at[n]).wait()

    def arrived(n, dst):
        pltpu.make_async_copy(dst, dst, a2a_recv.at[n]).wait()

    def z_slots(kappa, part):
        return pl.ds(HALF * kappa + QUART * part, QUART)

    def gather_copy(kappa, f, s):
        direction, part, _ = FLOWS[f]
        block = lbuf.at[zs[-direction * s % NZ], z_slots(kappa, part)]
        return pltpu.make_async_remote_copy(
            src_ref=block, dst_ref=block,
            send_sem=ag_send.at[kappa, f, s], recv_sem=ag_recv.at[kappa, f, s],
            device_id=z_id(direction), device_id_type=MESH,
        )

    def gather_start(kappa):
        for f in range(NF):
            gather_copy(kappa, f, 0).start()

    def gather_pump(kappa, s):
        for f in range(NF):
            if s < FLOWS[f][2]:
                gather_copy(kappa, f, s).wait_recv()
                if s + 1 < FLOWS[f][2]:
                    gather_copy(kappa, f, s + 1).start()

    def unmix_left(kappa, zz):
        for n in range(4):
            ylk, q = n // 2, n % 2
            x = [lbuf[zz, HALF * kappa + (4 * q + t) * 2 + ylk].astype(F32) for t in range(4)]
            y = exchange4(x)
            k0 = pl.multiple_of((ylk * NZ + zz) * 32, 32)
            lanes = pl.ds(256 * kappa + q * 128, 128)
            for h in range(HS):
                block = cat([y[b][8 * h : 8 * h + 8] for b in range(4)])
                lm[h, pl.ds(k0, 32), lanes] = block.astype(BF16)

    def unmix_gathered(kappa, s):
        if s < 3:
            unmix_left(kappa, zs[NZ - s - 1])
            unmix_left(kappa, zs[s + 1])
        else:
            unmix_left(kappa, zs[4])

    def unmix_pair(src, first, count, put):
        for m in range(count):
            y = swap64(src[first + 2 * m].astype(F32), src[first + 2 * m + 1].astype(F32))
            for h in range(HS):
                put(h, m, cat([y[g][16 * h : 16 * h + 16] for g in range(2)]).astype(BF16))

    def unmix_right():
        for kappa in range(2):

            def put(h, m, block):
                rm[h, pl.ds((2 * m + kappa) * 32, 32), :] = block

            unmix_pair(rbuf, HALF * kappa, 8, put)

    def unmix_d(kappa):
        def put(h, m, block):
            dm[h, pl.ds(256 * kappa + m * 32, 32), :] = block

        unmix_pair(dbuf, HALF * kappa, 8, put)

    def mix_pair(per_channel, blocks, put):
        for m in range(blocks):
            for h in range(HS):
                r0 = h * per_channel + m * 32
                y = swap64(scr[pl.ds(r0, 16), :], scr[pl.ds(r0 + 16, 16), :])
                for v in range(2):
                    put(m, v, h, y[v].astype(BF16))

    def triangle(kappa):
        for h in range(HS):
            scr[256 * h : 256 * h + 256, :] = dot_nn(rmt[h], lm[h, :, 256 * kappa : 256 * kappa + 256]).T

        def put(m, v, h, block):
            tsend[kappa, 2 * m + v, 16 * h : 16 * h + 16, :] = block

        mix_pair(256, 8, put)
        part_start(2 + kappa, kappa, tsend.at[kappa], tbuf)

    for load in small_loads:
        load.wait()
    g_in, b_in, g_tri, b_tri = gain[...], bias[...], o_gain[...], o_bias[...]
    wg, wo = w_gate[...], w_out[...]

    def slab(kappa, n):
        @pl.when(core == kappa)
        def _():
            if n == 0:
                arrived(2 + kappa, tbuf)
                scr[...] = tbuf[...].reshape(2048, 128).astype(F32)
            slab_back(n, scr, scr2, up_s, tri_s)
            if n == 1:
                dsend[...] = scr2[...].astype(BF16).reshape(PLANE, 64, 128)
                all_start(4 + kappa, dsend, dbuf, me)

    def sum_copy(kappa, f, s):
        direction, part, steps = FLOWS[f]
        block = dls.at[zs[direction * (steps - s) % NZ], z_slots(kappa, part)]
        return pltpu.make_async_remote_copy(
            src_ref=block, dst_ref=rsbuf.at[kappa, f, s],
            send_sem=rs_send.at[kappa, f, s], recv_sem=rs_recv.at[kappa, f, s],
            device_id=z_id(direction), device_id_type=MESH,
        )

    def left_sums(kappa):
        arrived(4 + kappa, dbuf.at[pl.ds(HALF * kappa, HALF)])
        unmix_d(kappa)
        for h in range(HS):
            big[h] = dot_nt(rm[h], dm[h, 256 * kappa : 256 * kappa + 256, :])

        def pack(zz):
            for ylk in range(2):
                k0 = pl.multiple_of((ylk * NZ + zz) * 32, 32)
                for q in range(2):
                    x = [
                        cat([big[h, pl.ds(k0 + 8 * b, 8), 128 * q : 128 * q + 128] for h in range(HS)])
                        for b in range(4)
                    ]
                    y = exchange4(x)
                    for t in range(4):
                        dls[zz, HALF * kappa + (4 * q + t) * 2 + ylk] = y[t].astype(BF16)

        for k in (4, 3, 5):
            pack(zs[k])
            for f in range(NF):
                direction, _, steps = FLOWS[f]
                if direction * steps % NZ == k:
                    sum_copy(kappa, f, 0).start()
        for k in (2, 6, 1, 7, 0):
            pack(zs[k])

    def sum_pump(kappa, s):
        for f in range(NF):
            direction, part, steps = FLOWS[f]
            if s < steps:
                sum_copy(kappa, f, s).wait_recv()
                if s + 1 < steps:
                    here = (zs[direction * (steps - s - 1) % NZ], z_slots(kappa, part))
                    dls[here] = (dls[here].astype(F32) + rsbuf[kappa, f, s].astype(F32)).astype(BF16)
                    sum_copy(kappa, f, s + 1).start()

    def left_out(kappa):
        for part in range(4):
            total = dls[z, z_slots(kappa, part)].astype(F32)
            for f in range(NF):
                if FLOWS[f][1] == part:
                    total = total + rsbuf[kappa, f, FLOWS[f][2] - 1].astype(F32)
            dlsend[kappa, QUART * part : QUART * part + QUART] = total.astype(BF16)
        part_start(7 + kappa, kappa, dlsend.at[kappa], dlbuf)

    loads[0].wait()
    project_left(left, g_in, b_in, w_left[...], ls, lfac, scr)
    pl.semaphore_wait(barrier, PLANE - 1 + 2)
    @pl.when(core == 0)
    def _():
        all_start(0, ls, lbuf.at[z], me)

    loads[1].wait()
    project_right(right, g_in, b_in, w_right[...], rs, rfac, scr2)

    @pl.when(core == 1)
    def _():
        all_start(9, ls, lbuf.at[z], me)

    loads[2].wait()
    loads[3].wait()
    gate_rows(pair_out, cot, g_in, b_in, wg, wo, g_tri, gate_s, std_s, inv_s, up_s)
    arrived(0, lbuf.at[z, pl.ds(0, HALF)])
    gather_start(0)
    unmix_left(0, z)
    gather_pump(0, 0)
    arrived(9, lbuf.at[z, pl.ds(HALF, HALF)])
    gather_start(1)
    all_start(1, rs, rbuf, me)
    unmix_left(1, z)
    unmix_gathered(0, 0)
    gather_pump(0, 1)
    gather_pump(1, 0)
    unmix_gathered(0, 1)
    unmix_gathered(1, 0)
    gather_pump(0, 2)
    gather_pump(1, 1)
    arrived(1, rbuf)
    unmix_right()
    for h in range(HS):
        rmt[h] = rm[h].T
    unmix_gathered(0, 2)
    gather_pump(0, 3)
    unmix_gathered(0, 3)

    triangle(0)
    gather_pump(1, 2)
    unmix_gathered(1, 1)
    unmix_gathered(1, 2)
    gather_pump(1, 3)
    unmix_gathered(1, 3)
    triangle(1)

    slab(0, 0)
    slab(0, 1)
    slab(1, 0)
    slab(1, 1)
    left_sums(0)
    left_sums(1)
    sum_pump(0, 0)
    sum_pump(1, 0)
    for h in range(HS):
        scr[512 * h : 512 * h + 512, :] = dot_nn(lm[h], dm[h])

    def put_right(m, v, h, block):
        drsend[(m % 2) * HALF + (m // 2) * 2 + v, 16 * h : 16 * h + 16, :] = block

    mix_pair(512, 16, put_right)
    all_start(6, drsend, drbuf, me)
    sum_pump(0, 1)
    sum_pump(1, 1)
    slab_rows(cot, g_in, g_tri, b_tri, wg, wo, gate_s, std_s, inv_s, tri_s, result, grad_out)
    stores[0].start()
    stores[1].start()
    prepare_left(left, lstd, linv)
    sum_pump(0, 2)
    sum_pump(1, 2)
    sum_pump(0, 3)
    left_out(0)
    sum_pump(1, 3)
    left_out(1)
    arrived(6, drbuf)
    scr[...] = drbuf[...].reshape(2048, 128).astype(F32)
    wr = w_right[...]
    back_right(0, right, rfac, g_in, wr, grad_right, scr)
    back_right(1, right, rfac, g_in, wr, grad_right, scr)
    stores[3].start()
    for kappa in range(2):

        @pl.when(core == kappa)
        def _():
            arrived(7 + kappa, dlbuf)

    scr[0:1024, :] = dlbuf[...].reshape(1024, 128).astype(F32)
    back_left(lstd, linv, lfac, g_in, w_left[...], grad_left, scr)
    stores[2].start()

    for kappa in range(2):

        @pl.when(core == kappa)
        def _():
            all_drain(9 * kappa, ls)

    all_drain(1, rs)
    all_drain(6, drsend)
    for kappa in range(2):
        part_drain(2 + kappa, kappa, tsend.at[kappa])
        part_drain(7 + kappa, kappa, dlsend.at[kappa])

        @pl.when(core == kappa)
        def _():
            all_drain(4 + kappa, dsend)

        for f in range(NF):
            for s in range(FLOWS[f][2]):
                gather_copy(kappa, f, s).wait_send()
                sum_copy(kappa, f, s).wait_send()
    for store in stores:
        store.wait()


def hand_over_kernel(*refs):
    srcs, dsts, held = refs[:4], refs[4:8], refs[8:12]
    in_sem, out_sem = refs[12:]
    pieces = [(n, p) for p in range(2) for n in range(4)]

    def copy(froms, tos, sems, n, p):
        rows = pl.ds(16 * p, 16)
        return pltpu.make_async_copy(froms[n].at[rows], tos[n].at[rows], sems.at[n, p])

    for n, p in pieces:
        copy(srcs, held, in_sem, n, p).start()
    for n, p in pieces:
        copy(srcs, held, in_sem, n, p).wait()
        copy(held, dsts, out_sem, n, p).start()
    for n, p in pieces:
        copy(held, dsts, out_sem, n, p).wait()


VMEM_LIMIT = 56 * 1024 * 1024


def per_device(
    pair_out, pair_left, pair_right, ln_gain, ln_bias, w_left, w_right, w_gate, w_out,
    out_gain, out_bias, cotangent,
):
    hbm = pl.BlockSpec(memory_space=pl.ANY)
    gain, bias = ln_gain.reshape(1, 128), ln_bias.reshape(1, 128)
    o_gain, o_bias = out_gain.reshape(1, 128), out_bias.reshape(1, 128)

    def vmem(*shape, dtype=BF16):
        return pltpu.VMEM(shape, dtype)

    def wide(*shape):
        return pltpu.VMEM(shape, F32)

    pair, lefts = (32, 48, 128), (32, 32, 128)
    small = [wide(1, 128), wide(1, 128), vmem(128, 256), vmem(128, 256)]
    small += [vmem(128, 128), vmem(128, 128), wide(1, 128), wide(1, 128)]
    slots, half_slots = vmem(PLANE, 64, 128), vmem(PLANE, 32, 128)
    dma = pltpu.SemaphoreType.DMA
    outs = tuple(jax.ShapeDtypeStruct(shape, BF16) for shape in (pair, pair, lefts, pair))
    made = pl.pallas_call(
        triangle_kernel,
        out_shape=outs,
        in_specs=[hbm] * 12,
        out_specs=(hbm,) * 4,
        scratch_shapes=small + [
            vmem(*lefts), vmem(*pair), vmem(*pair), vmem(*pair),
            vmem(*pair), vmem(*pair), vmem(*lefts), vmem(*pair),
            half_slots, slots,
            wide(8, 256, 128), wide(16, 256, 128),
            wide(1536, 128), wide(1536, 128), wide(1536, 128),
            wide(1536, 128), wide(1536, 128), wide(1024, 128), wide(1024, 128),
            vmem(NZ, PLANE, 32, 128), slots,
            vmem(2, HALF, 64, 128), slots,
            slots, slots,
            slots, slots,
            vmem(NZ, PLANE, 32, 128), vmem(2, NF, 4, QUART, 32, 128),
            vmem(2, HALF, 32, 128), half_slots,
            vmem(HS, 512, 512), vmem(HS, 512, 128),
            vmem(HS, 128, 512), vmem(HS, 512, 128),
            wide(2048, 128), wide(2048, 128), wide(HS, 512, 256),
            dma((8,)), dma((4,)), dma((4,)), dma((10,)), dma((10,)),
            dma((2, NF, 4)), dma((2, NF, 4)), dma((2, NF, 4)), dma((2, NF, 4)),
        ],
        compiler_params=pltpu.CompilerParams(
            vmem_limit_bytes=VMEM_LIMIT, collective_id=0, has_side_effects=True
        ),
        name="triangle",
    )(
        pair_left, pair_right, pair_out, cotangent, gain, bias, w_left, w_right, w_gate, w_out,
        o_gain, o_bias,
    )
    return pl.pallas_call(
        hand_over_kernel,
        out_shape=outs,
        in_specs=[hbm] * 4,
        out_specs=(hbm,) * 4,
        scratch_shapes=[vmem(*pair), vmem(*pair), vmem(*lefts), vmem(*pair), dma((4, 2)), dma((4, 2))],
        compiler_params=pltpu.CompilerParams(vmem_limit_bytes=VMEM_LIMIT),
        name="hand_over",
    )(*made)


def solution(mesh):
    pairs, lefts = P("row", "col", None), P("col", "row", None)
    return jax.shard_map(
        per_device,
        mesh=mesh,
        in_specs=(pairs, lefts, pairs, P(), P(), P(), P(), P(), P(), P(), P(), pairs),
        out_specs=(pairs, pairs, lefts, pairs),
        check_vma=False,
    )
```
